256 devices in a mesh: seq: 16 (over x_hi, z), tp: 8 (over x_lo, y), role: 2 (over core).
Axes of the slice: x: 4 (x_hi: 2, x_lo: 2; x = x_hi * 2 + x_lo), y: 4, z: 8, core: 2. Of those that a mesh axis runs over, the one named last changes fastest.
Arguments:
- prompt_length: int32 [2], P('role'), may hold values from 3073 to 4096, as said below
- owner_map: int32 [8], replicated, may hold values from 0 to 7, as said below
- queries: bfloat16 [2, 4096, 8192], P('role', 'seq', 'tp'), may hold values from -6 to 6
- key_rows: bfloat16 [2, 4096, 1024], P('role', 'seq', 'tp'), may hold values from -6 to 6
- value_matrix: bfloat16 [2, 4096, 1024], P('role', 'seq', 'tp'), may hold values from -6 to 6
- ssm_input: bfloat16 [2, 4096, 16384], P('role', 'seq', 'tp'), may hold values from -6 to 6
- gate_input: bfloat16 [2, 4096, 16384], P('role', 'seq', 'tp'), may hold values from -6 to 6
- step_sizes: bfloat16 [2, 4096, 256], P('role', 'seq', 'tp'), may hold values from 0.049804688 to 0.19921875
- decay_rate: float32 [256], P('tp'), may hold values from 0 to 1
- skip_gain: float32 [256], P('tp'), may hold values from 0.5 to 1.5
- write_proj: bfloat16 [2, 4096, 2048], P('role', 'seq', 'tp'), may hold values from -0.59765625 to 0.59765625
- read_proj: bfloat16 [2, 4096, 2048], P('role', 'seq', 'tp'), may hold values from -0.59765625 to 0.59765625
- norm_gain: float32 [16384], P('tp'), may hold values from 0.1 to 1.9
Outputs:
- mamba_out: bfloat16 [2, 4096, 16384], P('role', 'seq', 'tp')
- attn_out: bfloat16 [2, 4096, 8192], P('role', 'seq', 'tp')
- decode_state: float32 [2, 256, 64, 256], P('role', ('tp', 'seq'))
- decode_kv: bfloat16 [2, 2, 4096, 1024], P('role', None, 'seq', 'tp')
The draws below stay inside these ranges and needn't reach their ends.
Inputs may be any that keep to these rules, and one draw needn't show every extreme that they name: `prompt_length`: one of the two requests fills all 4096 positions. owner_map[b] = b XOR k for one k from 1 to 7.
All inputs are finite; a program needn't handle non-finite values.
Results may differ from the reference program's by a relative error of at most 0.008.
Values may be sent and summed in bfloat16 or wider, within the bound.
A program may use at most 128 MiB of HBM per device.

```python
import math
import jax
import jax.numpy as jnp
from jax import lax

MH = 256
P_SIZE = 64
N = 256
GROUPS = 8
QUERY_HEADS = 64
KEY_VALUE_HEADS = 8
HEAD_WIDTH = 128
SPAN = 128
REQUEST_TOKENS = 4096
BLOCKS = 8
KV_LOCAL = 1
N_TP = 8


def draw_prompt_length(key, part):
    full_index = jax.random.randint(jax.random.fold_in(key, 11), (), 0, 2)
    shorter = REQUEST_TOKENS - jax.random.randint(jax.random.fold_in(key, 12), (), 0, REQUEST_TOKENS // 4)
    return jnp.where(jnp.arange(2) == full_index, REQUEST_TOKENS, shorter).astype(jnp.int32)


def draw_owner_map(key, part):
    key = jax.random.fold_in(key, 27)
    choices_list = jax.random.permutation(key, jnp.arange(1, BLOCKS, dtype=jnp.int32))
    offset = choices_list[0].astype(jnp.int32)
    return jnp.bitwise_xor(jnp.arange(BLOCKS, dtype=jnp.int32), offset)


def draw_decay_rate(key, part):
    share = 0.5
    quick = jax.random.uniform(jax.random.fold_in(key, 31), (MH,)) < share
    fast_rate = jnp.exp(jax.random.uniform(jax.random.fold_in(key, 32), (MH,), minval=jnp.log(0.2), maxval=jnp.log(0.35)))
    slow_rate = jnp.exp(jax.random.uniform(jax.random.fold_in(key, 33), (MH,), minval=jnp.log(2.0 / REQUEST_TOKENS), maxval=jnp.log(16.0 / REQUEST_TOKENS)))
    return jnp.where(quick, fast_rate, slow_rate).astype(jnp.float32)


def draw_queries(key, part):
    base_offset = jnp.clip(jax.random.normal(jax.random.fold_in(key, 42), (2, REQUEST_TOKENS, QUERY_HEADS * HEAD_WIDTH)), -6.0, 6.0)
    return base_offset.astype(jnp.bfloat16)


def draw_key_rows(key, part):
    base_offset = jnp.clip(jax.random.normal(jax.random.fold_in(key, 43), (2, REQUEST_TOKENS, KEY_VALUE_HEADS * HEAD_WIDTH)), -6.0, 6.0)
    return base_offset.astype(jnp.bfloat16)


def levels(rng, shape, cuts, low, high):
    def one(axis_at, shards_of):
        steps = jax.random.uniform(jax.random.fold_in(jax.random.fold_in(rng, 6), axis_at), (shards_of,), jnp.float32, low / len(cuts), high / len(cuts))
        return jnp.repeat(jnp.exp(steps), shape[axis_at] // shards_of).reshape((-1,) + (1,) * (len(shape) - axis_at - 1))

    level = one(*cuts[0])
    for cut in cuts[1:]:
        level = level * one(*cut)
    return level


def scatter_about(own_key, shape, scale, reach, cuts=(), held_as=jnp.bfloat16):
    values = jax.random.normal(own_key, shape, jnp.float32) * scale
    if len(cuts) > 0:
        values = levels(own_key, shape, cuts, -0.22, 0.18) * values
    return jnp.clip(values, min=-reach, max=reach).astype(held_as)


def setup_inputs(seed: int = 0) -> dict:
    keys = jax.random.split(jax.random.key(seed), 14)
    return {
        "prompt_length": draw_prompt_length(jax.random.fold_in(keys[13], 71), 0),
        "owner_map": draw_owner_map(jax.random.fold_in(keys[13], 71), 0),
        "queries": draw_queries(jax.random.fold_in(keys[13], 71), 0),
        "key_rows": draw_key_rows(jax.random.fold_in(keys[13], 71), 0),
        "value_matrix": scatter_about(keys[4], (2, REQUEST_TOKENS, KEY_VALUE_HEADS * HEAD_WIDTH), 1.0, 6.0, ((0, 2), (1, 16), (2, 8))),
        "ssm_input": scatter_about(keys[5], (2, REQUEST_TOKENS, MH * P_SIZE), 1.0, 6.0, ((0, 2), (1, 16), (2, 8))),
        "gate_input": scatter_about(keys[6], (2, REQUEST_TOKENS, MH * P_SIZE), 1.0, 6.0, ((0, 2), (1, 16), (2, 8))),
        "step_sizes": jnp.clip(jnp.exp(math.log(0.19921875) - 1.3862944 * jax.random.uniform(keys[7], (2, REQUEST_TOKENS, MH), jnp.float32) ** levels(keys[7], (2, REQUEST_TOKENS, MH), ((0, 2), (1, 16), (2, 8)), -0.2, 0.2)), 0.049804688, 0.19921875).astype(jnp.bfloat16),
        "decay_rate": draw_decay_rate(jax.random.fold_in(keys[13], 71), 0),
        "skip_gain": jnp.clip(0.5 + 1.0 * jax.random.uniform(keys[9], (MH,), jnp.float32) ** levels(keys[9], (MH,), ((0, 8),), -0.2, 0.2), 0.5, 1.5),
        "write_proj": scatter_about(keys[10], (2, REQUEST_TOKENS, GROUPS * N), 0.1, 0.59765625, ((0, 2), (1, 16), (2, 8))),
        "read_proj": scatter_about(keys[11], (2, REQUEST_TOKENS, GROUPS * N), 0.1, 0.59765625, ((0, 2), (1, 16), (2, 8))),
        "norm_gain": jnp.clip(1.0 + 0.18 * jax.random.normal(keys[12], (MH * P_SIZE,), jnp.float32), 0.1, 1.9),
    }


precise = lax.Precision.HIGHEST

def span_core(input_matrix, step_heads, head_rates, write_rows, read_rows, start_state):
    running = jnp.cumsum(-step_heads * head_rates[..., None], axis=-1)
    span_rows = input_matrix.shape[0]
    causal = jnp.arange(span_rows)[:, None] >= jnp.arange(span_rows)[None, :]
    spread = running[..., :, None] - running[..., None, :]
    damping = jnp.where(causal, jnp.exp(jnp.where(causal, spread, 0.0)), 0.0)
    intersection = jnp.einsum('tgn,sgn->gts', read_rows, write_rows, preferred_element_type=jnp.float32)
    mixer_kind = (intersection[:, None] * damping * step_heads[..., None, :]).astype(jnp.bfloat16)
    inner_portion = jnp.einsum('wuhy,ywue->hwue', mixer_kind, input_matrix, preferred_element_type=jnp.float32)
    carried = jnp.einsum('tgn,grpn->tgrp', read_rows, start_state.astype(jnp.bfloat16), preferred_element_type=jnp.float32)
    carried = carried * jnp.moveaxis(jnp.exp(running), -1, 0)[..., None]
    tail_weight = jnp.exp(running[..., -1:] - running) * step_heads
    weighted = (input_matrix.astype(jnp.float32) * jnp.moveaxis(tail_weight, -1, 0)[..., None]).astype(jnp.bfloat16)
    fresh_part = jnp.einsum('sgrp,sgn->grpn', weighted, write_rows, preferred_element_type=jnp.float32)
    updated = start_state * jnp.exp(running[..., -1])[..., None, None] + fresh_part
    return (inner_portion + carried, updated)

def scan_spans(input_matrix, step_heads, head_rates, write_rows, read_rows, start_state):
    row_total = input_matrix.shape[0]
    span_count = row_total // SPAN
    groups_here = step_heads.shape[0]
    heads_here = step_heads.shape[1]
    input_spans = input_matrix.reshape((span_count, SPAN) + input_matrix.shape[1:])
    step_spans = jnp.moveaxis(step_heads.reshape(groups_here, heads_here, span_count, SPAN), 2, 0)
    write_spans = write_rows.reshape((span_count, SPAN) + write_rows.shape[1:])
    read_spans = read_rows.reshape((span_count, SPAN) + read_rows.shape[1:])

    def advance(carried_state, pieces):
        mixed_rows, next_state = span_core(pieces[0], pieces[1], head_rates, pieces[2], pieces[3], carried_state)
        return (next_state, mixed_rows)
    final_state, mixed_spans = lax.scan(advance, start_state, (input_spans, step_spans, write_spans, read_spans))
    return (mixed_spans.reshape((row_total,) + mixed_spans.shape[2:]), final_state)

def attention_layer(query_matrix, key_portion, value_portion, length):
    row_total = query_matrix.shape[0]
    heads_per_group = QUERY_HEADS // KEY_VALUE_HEADS
    heads_of_query = query_matrix.astype(jnp.float32).reshape(row_total, KEY_VALUE_HEADS, heads_per_group, HEAD_WIDTH)
    heads_of_key = key_portion.astype(jnp.float32).reshape(row_total, KEY_VALUE_HEADS, HEAD_WIDTH)
    heads_of_value = value_portion.astype(jnp.float32).reshape(row_total, KEY_VALUE_HEADS, HEAD_WIDTH)
    block_rows = math.gcd(row_total, 256)
    positions = jnp.arange(row_total, dtype=jnp.int32)

    def one_block(block_index):
        first_row = block_index * block_rows
        query_block = lax.dynamic_slice_in_dim(heads_of_query, first_row, block_rows, 0)
        scores = jnp.einsum('tkrd,skd->krts', query_block, heads_of_key, precision=precise) * HEAD_WIDTH ** (-0.5)
        query_pos = first_row + jnp.arange(block_rows, dtype=jnp.int32)
        allowed = positions[None, :] <= query_pos[:, None]
        scores = jnp.where(allowed, scores, -jnp.inf)
        row_top = lax.optimization_barrier(jnp.max(scores, axis=-1, keepdims=True))
        weights = jnp.exp(scores - row_top)
        denominator = lax.optimization_barrier(jnp.sum(weights, axis=-1))
        rounded = lax.optimization_barrier(weights.astype(jnp.bfloat16)).astype(jnp.float32)
        mixed = jnp.einsum('krts,skd->krtd', rounded, heads_of_value, precision=precise)
        return jnp.moveaxis(mixed / denominator[..., None], 2, 0)
    block_outs = lax.map(one_block, jnp.arange(row_total // block_rows, dtype=jnp.int32))
    attended = block_outs.reshape(row_total, QUERY_HEADS * HEAD_WIDTH)
    live_rows = positions < length
    return jnp.where(live_rows[:, None], attended, 0.0).astype(jnp.bfloat16)

def mamba_layer(inputs, gates, steps_in, rates, skips, writes, reads, gains, length):
    row_total = inputs.shape[0]
    heads_group = MH // GROUPS
    live_rows = jnp.arange(row_total, dtype=jnp.int32) < length
    step_live = jnp.where(live_rows[:, None], steps_in.astype(jnp.float32), 0.0)
    step_heads = step_live.T.reshape(GROUPS, heads_group, row_total)
    shaped = inputs.reshape(row_total, GROUPS, heads_group, P_SIZE)
    start_state = jnp.zeros((GROUPS, heads_group, P_SIZE, N), jnp.float32)
    mixed_rows, final_state = scan_spans(shaped, step_heads, rates.reshape(GROUPS, heads_group), writes.reshape(row_total, GROUPS, N), reads.reshape(row_total, GROUPS, N), start_state)
    with_skip = mixed_rows + skips.reshape(GROUPS, heads_group)[None, :, :, None] * shaped.astype(jnp.float32)
    ssm_out = with_skip.reshape(row_total, MH * P_SIZE).astype(jnp.bfloat16)
    gated = ssm_out.astype(jnp.float32) * jax.nn.silu(gates.astype(jnp.float32))
    grouped = gated.reshape(row_total, GROUPS, heads_group * P_SIZE)
    normed = grouped * lax.rsqrt(lax.optimization_barrier(jnp.mean(grouped * grouped, axis=-1, keepdims=True)) + 1e-05)
    result = normed.reshape(row_total, MH * P_SIZE) * gains[None, :]
    result = jnp.where(live_rows[:, None], result, 0.0).astype(jnp.bfloat16)
    return (result, final_state.reshape(MH, P_SIZE, N))

def reference(prompt_length, owner_map, queries, key_rows, value_matrix, ssm_input, gate_input, step_sizes, decay_rate, skip_gain, write_proj, read_proj, norm_gain):
    mamba_list = []
    attn_list = []
    state_list = []
    cache_entries = []
    tp_owner = owner_map[::KV_LOCAL] // KV_LOCAL
    for request in range(2):
        length = prompt_length[request]
        mamba_rows, final_state = mamba_layer(ssm_input[request], gate_input[request], step_sizes[request], decay_rate, skip_gain, write_proj[request], read_proj[request], norm_gain, length)
        mamba_list.append(mamba_rows)
        attn_list.append(attention_layer(queries[request], key_rows[request], value_matrix[request], length))
        state_blocks = final_state.reshape(N_TP, MH // N_TP, P_SIZE, N)
        moved_state = jnp.zeros_like(state_blocks).at[tp_owner].set(state_blocks)
        state_list.append(moved_state.reshape(MH, P_SIZE, N))
        live_rows = jnp.arange(REQUEST_TOKENS, dtype=jnp.int32) < length
        stacked_rows = jnp.stack([key_rows[request], value_matrix[request]])
        stacked_rows = jnp.where(live_rows[None, :, None], stacked_rows, jnp.zeros((), jnp.bfloat16))
        key_value_blocks = stacked_rows.reshape(2, REQUEST_TOKENS, KEY_VALUE_HEADS, HEAD_WIDTH)
        moved_key_value = jnp.zeros_like(key_value_blocks).at[:, :, owner_map].set(key_value_blocks)
        cache_entries.append(moved_key_value.reshape(2, REQUEST_TOKENS, KEY_VALUE_HEADS * HEAD_WIDTH))
    mamba_out = jnp.stack(mamba_list)
    attn_out = jnp.stack(attn_list)
    decode_state = jnp.stack([state_list[1], state_list[0]])
    decode_kv = jnp.stack([cache_entries[1], cache_entries[0]])
    return (mamba_out, attn_out, decode_state, decode_kv)
```

```python
import jax
import jax.numpy as jnp
from jax import lax
from jax.experimental import pallas as pl
from jax.experimental.pallas import tpu as pltpu
from jax.sharding import PartitionSpec as P

MESH = pl.DeviceIdType.MESH
LOG2E = 1.4426950408889634
SCORE = 128**-0.5 * LOG2E
ROWS = 256
LANES = 128
SEQ = 16
RING = 8
HEADS = 8
STATE = 256
MSG = STATE + 16
F32 = jnp.float32
BF16 = jnp.bfloat16


def iota(shape, dim):
    return lax.broadcasted_iota(jnp.int32, shape, dim)


def pair_columns(table, pair):
    turned = pltpu.roll(table, lax.rem(LANES - 2 * pair, LANES), axis=1)
    low = iota(table.shape, 1) < 64
    return jnp.where(low, turned[:, 0:1], turned[:, 1:2])


def kernel(
    len_ref,
    own_ref,
    q_ref,
    k_ref,
    v_ref,
    x_ref,
    g_ref,
    st_ref,
    rate_ref,
    skip_ref,
    b_ref,
    c_ref,
    gain_ref,
    mo_ref,
    ao_ref,
    ds_ref,
    dk_ref,
    kvo,
    kvx,
    tx1,
    rx1,
    tx2,
    rx2,
    hkt,
    hkr,
    hst,
    hsr,
    log_ref,
    w_ref,
    e_ref,
    mt_ref,
    bt_ref,
    gm_ref,
    y_ref,
    el_ref,
    sg_ref,
    top_ref,
    acc_ref,
    state_ref,
    sq_ref,
    s1,
    r1,
    s2,
    r2,
    so,
    ro,
    sx,
    rx,
    sk,
    rk,
    sf,
    rf,
):
    s, t, r = lax.axis_index("seq"), lax.axis_index("tp"), lax.axis_index("role")
    row = s // RING
    z = lax.rem(s, RING)
    across = (lax.rem(s + RING, SEQ), t, r)

    def on_ring(step):
        return (row * RING + lax.rem(z + step + RING, RING), t, r)

    def owner_hop(level):
        if level == 0:
            return (s, t, 1 - r)
        width = 1 << (level - 1)
        return (s, t + width * (1 - 2 * lax.rem(t // width, 2)), r)

    def send(src, dst, ssem, rsem, device):
        return pltpu.make_async_remote_copy(
            src, dst, ssem, rsem, device_id=device, device_id_type=MESH
        )

    barrier = pltpu.get_barrier_semaphore()
    for k in range(1, SEQ):
        pl.semaphore_signal(
            barrier, inc=1, device_id=(lax.rem(s + k, SEQ), t, r), device_id_type=MESH
        )
    for level in range(4):
        pl.semaphore_signal(barrier, inc=1, device_id=owner_hop(level), device_id_type=MESH)

    length = len_ref[0]
    live = s * ROWS + iota((ROWS, LANES), 0) < length
    low = iota((ROWS, LANES), 1) < 64
    kvo[0, 0] = jnp.where(live, k_ref[0].astype(F32), 0.0).astype(BF16)
    kvo[0, 1] = jnp.where(live, v_ref[0].astype(F32), 0.0).astype(BF16)
    pl.semaphore_wait(barrier, SEQ - 1 + 4)

    def ring_copy(src, dst, device):
        return send(kvo.at[src], kvo.at[dst], so.at[dst], ro.at[dst], device)

    def cross_copy(slot):
        return send(kvo.at[slot], kvx.at[slot], sx.at[slot], rx.at[slot], across)

    def kv_hop(level):
        src = kvo.at[0] if level == 0 else hkt.at[level]
        return send(src, hkr.at[level], sk.at[level], rk.at[level], owner_hop(level))

    def state_hop(level):
        return send(
            hst.at[level], hsr.at[level], sf.at[level], rf.at[level], owner_hop(level)
        )

    def local_copy(k, device):
        return send(tx1.at[k], rx1.at[k], s1.at[k], r1.at[k], device)

    def prefix_copy(k, device):
        return send(tx2.at[k], rx2.at[k], s2.at[k], r2.at[k], device)

    ring_copy(0, RING - 1, on_ring(1)).start()
    ring_copy(0, 1, on_ring(-1)).start()

    @pl.when(row == 0)
    def _():
        cross_copy(0).start()

    kv_hop(0).start()

    steps = jnp.concatenate(
        [st_ref[0].astype(F32), jnp.zeros((ROWS, LANES - 32), F32)], axis=1
    )
    rates = jnp.concatenate([rate_ref[...], jnp.zeros((1, LANES - 32), F32)], axis=1)
    steps = jnp.where(live, steps, 0.0)
    causal = iota((ROWS, ROWS), 0) >= iota((ROWS, ROWS), 1)
    logs = jnp.dot(
        causal.astype(F32),
        steps * rates * -LOG2E,
        precision=lax.Precision.HIGHEST,
        preferred_element_type=F32,
    )
    used = steps > 0.0
    less = jnp.where(used, logs - jnp.log(jnp.where(used, steps, 1.0)) * LOG2E, 1e9)
    log_ref[...] = logs
    w_ref[...] = jnp.exp2(logs[ROWS - 1 :, :] - less)
    e_ref[...] = jnp.exp2(logs)
    mt_ref[...] = less.T
    bt_ref[...] = b_ref[0].astype(F32).T.astype(BF16)

    def local_state(k, carry):
        pair = lax.rem(s + k, SEQ)
        cols = pl.ds(pl.multiple_of(pair * LANES, LANES), LANES)
        weight = pair_columns(w_ref[...], pair)
        weighted = (x_ref[0, :, cols].astype(F32) * weight).astype(BF16)
        fresh = jnp.dot(bt_ref[...], weighted, preferred_element_type=F32)
        decay = pair_columns(e_ref[ROWS - 8 :, :], pair)[7:8, :]
        high = decay.astype(BF16).astype(F32)
        middle = (decay - high).astype(BF16).astype(F32)
        rest = decay - high - middle
        which = iota((16, LANES), 0)
        parts = jnp.where(
            which == 0, high, jnp.where(which == 1, middle, jnp.where(which == 2, rest, 0.0))
        )
        tx1[k, :STATE, :] = fresh.astype(BF16)
        tx1[k, STATE:, :] = parts.astype(BF16)

        @pl.when(k == 0)
        def _():
            rx1[0, :STATE, :] = fresh.astype(BF16)
            rx1[0, STATE:, :] = parts.astype(BF16)

        @pl.when(k > 0)
        def _():
            local_copy(k, (pair, t, r)).start()

        return carry

    lax.fori_loop(0, SEQ, local_state, 0)

    gm_ref[...] = jnp.where(
        causal,
        lax.dot_general(
            c_ref[0], b_ref[0], (((1,), (1,)), ((), ())), preferred_element_type=F32
        ),
        0.0,
    )

    def within(pair, carry):
        cols = pl.ds(pl.multiple_of(pair * LANES, LANES), LANES)
        turned = pltpu.roll(log_ref[...], lax.rem(LANES - 2 * pair, LANES), axis=1)
        columns = [jnp.broadcast_to(turned[:, i : i + 1], (ROWS, LANES)) for i in range(2)]
        lines = [mt_ref[pl.ds(2 * pair + i, 1), :] for i in range(2)]
        x = x_ref[0, :, cols].astype(F32)
        halves = [jnp.where(low, x, 0.0).astype(BF16), jnp.where(low, 0.0, x).astype(BF16)]

        def mix(head, down, right):
            rows, over = slice(down, down + 128), slice(right, right + 128)
            spread = columns[head][rows] - lines[head][:, over]
            return (gm_ref[rows, over] * jnp.exp2(spread)).astype(BF16)

        skips = jnp.concatenate([skip_ref[...], jnp.zeros((1, LANES - 32), F32)], axis=1)
        skipped = pair_columns(jnp.broadcast_to(skips, (8, LANES)), pair)[0:1, :] * x
        upper = jnp.dot(
            jnp.concatenate([mix(0, 0, 0), mix(1, 0, 0)], axis=1),
            jnp.concatenate([halves[0][:128], halves[1][:128]], axis=0),
            preferred_element_type=F32,
        )
        lower = jnp.dot(
            jnp.concatenate(
                [mix(0, 128, 0), mix(0, 128, 128), mix(1, 128, 0), mix(1, 128, 128)], axis=1
            ),
            jnp.concatenate(halves, axis=0),
            preferred_element_type=F32,
        )
        y_ref[:128, cols] = upper + skipped[:128]
        y_ref[128:, cols] = lower + skipped[128:]
        el_ref[:, cols] = jnp.exp2(jnp.where(low, columns[0], columns[1]))
        gate = g_ref[0, :, cols].astype(F32)
        sg_ref[:, cols] = gate / (1.0 + jnp.exp(-gate))
        return carry

    def attend(keys, values, diagonal):
        extended = jnp.concatenate([values, jnp.ones((ROWS, LANES), BF16)], axis=1)

        def head(h, carry):
            cols = pl.ds(pl.multiple_of(h * LANES, LANES), LANES)
            scores = lax.dot_general(
                q_ref[0, :, cols], keys, (((1,), (1,)), ((), ())), preferred_element_type=F32
            )
            scores = scores * SCORE
            if diagonal:
                scores = jnp.where(causal, scores, -jnp.inf)
            peak = jnp.max(scores, axis=1, keepdims=True)
            if diagonal:
                top = jnp.broadcast_to(peak, (ROWS, LANES))
            else:
                before = top_ref[h]
                top = jnp.maximum(before, peak)
            weights = jnp.concatenate(
                [jnp.exp2(scores[:, :LANES] - top), jnp.exp2(scores[:, LANES:] - top)], axis=1
            ).astype(BF16)
            part = jnp.dot(weights, extended, preferred_element_type=F32)
            top_ref[h] = top
            if diagonal:
                acc_ref[h] = part
            else:
                scale = jnp.exp2(before - top)
                acc_ref[h] = acc_ref[h] * jnp.concatenate([scale, scale], axis=1) + part
            return carry

        lax.fori_loop(0, HEADS, head, 0)

    attend(kvo[0, 0], kvo[0, 1], True)
    lax.fori_loop(0, 2, within, 0)

    key_xor = own_ref[0]

    def routed(level, arrived, held):
        bit = lax.rem(key_xor // (1 << (level - 1)), 2)
        take = jnp.broadcast_to(bit, arrived.shape) == 1
        return jnp.where(take, arrived.astype(F32), held.astype(F32)).astype(BF16)

    def kv_step(level):
        kv_hop(level).wait_recv()
        for part in range(2):
            moved = hkr[level, part]
            if level > 0:
                moved = routed(level, moved, hkt[level, part])
            if level < 3:
                hkt[level + 1, part] = moved
            else:
                dk_ref[0, part] = moved
        if level < 3:
            kv_hop(level + 1).start()

    def own_row(turn, carry):
        half = (turn + 1) // 2
        slot = jnp.where(lax.rem(turn, 2) == 1, RING - half, half)
        lax.fori_loop(2 * turn, 2 * turn + 2, within, 0)
        for level in range(4):

            @pl.when(turn == 2 * level + 1)
            def _():
                kv_step(level)

        ring_copy(0, slot, on_ring(1)).wait_recv()
        forward = slot >= 4

        @pl.when(jnp.logical_and(slot != 4, slot != 3))
        def _():
            step = jnp.where(forward, 1, -1)
            ring_copy(slot, slot - step, on_ring(step)).start()

        @pl.when(row == 0)
        def _():
            cross_copy(slot).start()

        @pl.when(lax.rem(z + slot, RING) < z)
        def _():
            attend(kvo[slot, 0], kvo[slot, 1], False)

        return carry

    lax.fori_loop(1, RING, own_row, 0)

    state_ref[...] = jnp.zeros((STATE, LANES), F32)

    def scan(i, carry):
        ahead = lax.rem(i - s + SEQ, SEQ)
        now = state_ref[...]
        tx2[ahead] = now.astype(BF16)

        @pl.when(ahead == 0)
        def _():
            rx2[0] = now.astype(BF16)

        @pl.when(ahead > 0)
        def _():
            prefix_copy(ahead, (i, t, r)).start()

        behind = lax.rem(s - i + SEQ, SEQ)

        @pl.when(behind > 0)
        def _():
            local_copy(behind, (i, t, r)).wait_recv()

        decay = jnp.sum(rx1[behind, STATE:, :].astype(F32), axis=0, keepdims=True)
        state_ref[...] = now * decay + rx1[behind, :STATE, :].astype(F32)
        return carry

    lax.fori_loop(0, SEQ, scan, 0)
    hst[0] = state_ref[...].astype(BF16)
    state_hop(0).start()

    def state_step(level):
        state_hop(level).wait_recv()
        moved = hsr[level]
        if level > 0:
            moved = routed(level, moved, hst[level])
        if level < 3:
            hst[level + 1] = moved
            state_hop(level + 1).start()
        else:
            ds_ref[0] = moved.astype(F32).T.reshape(2, 64, STATE)

    def other_row(turn, carry):
        half = (turn + 1) // 2
        slot = jnp.where(lax.rem(turn, 2) == 1, RING - half, half)

        @pl.when(row == 1)
        def _():
            cross_copy(slot).wait_recv()
            attend(kvx[slot, 0], kvx[slot, 1], False)

        for level in range(4):

            @pl.when(turn == 2 * level + 1)
            def _():
                state_step(level)

        return carry

    lax.fori_loop(0, RING, other_row, 0)

    def finish(h, carry):
        cols = pl.ds(pl.multiple_of(h * LANES, LANES), LANES)
        both = acc_ref[h]
        ao_ref[0, :, cols] = jnp.where(live, both[:, :LANES] / both[:, LANES:], 0.0).astype(BF16)
        return carry

    lax.fori_loop(0, HEADS, finish, 0)

    sq_ref[...] = jnp.zeros((ROWS, LANES), F32)

    def outputs(k, carry):
        pair = lax.rem(s - k + SEQ, SEQ)
        cols = pl.ds(pl.multiple_of(pair * LANES, LANES), LANES)

        @pl.when(k > 0)
        def _():
            prefix_copy(k, (pair, t, r)).wait_recv()

        carried = jnp.dot(c_ref[0], rx2[k], preferred_element_type=F32)
        mixed = (y_ref[:, cols] + el_ref[:, cols] * carried).astype(BF16).astype(F32)
        gated = mixed * sg_ref[:, cols]
        y_ref[:, cols] = gated
        sq_ref[...] += gated * gated
        return carry

    lax.fori_loop(0, SEQ, outputs, 0)
    mean = jnp.sum(sq_ref[...], axis=1, keepdims=True) * (1.0 / 2048.0)
    factor = jnp.where(live, lax.rsqrt(mean + 1e-05), 0.0)

    def norm(pair, carry):
        cols = pl.ds(pl.multiple_of(pair * LANES, LANES), LANES)
        mo_ref[0, :, cols] = (y_ref[:, cols] * factor * gain_ref[:, cols]).astype(BF16)
        return carry

    lax.fori_loop(0, SEQ, norm, 0)

    def sent(k, carry):
        local_copy(k, (lax.rem(s + k, SEQ), t, r)).wait_send()
        prefix_copy(k, (lax.rem(s + k, SEQ), t, r)).wait_send()
        return carry

    lax.fori_loop(1, SEQ, sent, 0)
    for slot in range(1, RING):
        ring_copy(0, slot, on_ring(1)).wait_send()

    @pl.when(row == 0)
    def _():
        for slot in range(RING):
            cross_copy(slot).wait_send()

    for level in range(4):
        kv_hop(level).wait_send()
        state_hop(level).wait_send()


def on_device(
    prompt_length,
    owner_map,
    queries,
    key_rows,
    value_matrix,
    ssm_input,
    gate_input,
    step_sizes,
    decay_rate,
    skip_gain,
    write_proj,
    read_proj,
    norm_gain,
):
    smem = pl.BlockSpec(memory_space=pltpu.SMEM)
    vmem = pl.BlockSpec(memory_space=pltpu.VMEM)
    dma = pltpu.SemaphoreType.DMA
    wide = pltpu.VMEM((ROWS, SEQ * LANES), F32)
    square = pltpu.VMEM((ROWS, LANES), F32)
    return pl.pallas_call(
        kernel,
        name="prefill",
        out_shape=(
            jax.ShapeDtypeStruct((1, ROWS, 2048), BF16),
            jax.ShapeDtypeStruct((1, ROWS, 1024), BF16),
            jax.ShapeDtypeStruct((1, 2, 64, STATE), F32),
            jax.ShapeDtypeStruct((1, 2, ROWS, LANES), BF16),
        ),
        in_specs=[smem, smem] + [vmem] * 11,
        out_specs=(vmem,) * 4,
        scratch_shapes=[
            pltpu.VMEM((RING, 2, ROWS, LANES), BF16),
            pltpu.VMEM((RING, 2, ROWS, LANES), BF16),
            pltpu.VMEM((SEQ, MSG, LANES), BF16),
            pltpu.VMEM((SEQ, MSG, LANES), BF16),
            pltpu.VMEM((SEQ, STATE, LANES), BF16),
            pltpu.VMEM((SEQ, STATE, LANES), BF16),
            pltpu.VMEM((4, 2, ROWS, LANES), BF16),
            pltpu.VMEM((4, 2, ROWS, LANES), BF16),
            pltpu.VMEM((4, STATE, LANES), BF16),
            pltpu.VMEM((4, STATE, LANES), BF16),
            square,
            square,
            square,
            pltpu.VMEM((LANES, ROWS), F32),
            pltpu.VMEM((STATE, ROWS), BF16),
            pltpu.VMEM((ROWS, ROWS), F32),
            wide,
            wide,
            wide,
            pltpu.VMEM((HEADS, ROWS, LANES), F32),
            pltpu.VMEM((HEADS, ROWS, 2 * LANES), F32),
            pltpu.VMEM((STATE, LANES), F32),
            square,
            dma((SEQ,)),
            dma((SEQ,)),
            dma((SEQ,)),
            dma((SEQ,)),
            dma((RING,)),
            dma((RING,)),
            dma((RING,)),
            dma((RING,)),
            dma((4,)),
            dma((4,)),
            dma((4,)),
            dma((4,)),
        ],
        compiler_params=pltpu.CompilerParams(
            collective_id=0, has_side_effects=True, vmem_limit_bytes=48 * 2**20
        ),
    )(
        prompt_length,
        owner_map,
        queries,
        key_rows,
        value_matrix,
        ssm_input,
        gate_input,
        step_sizes,
        decay_rate.reshape(1, 32),
        skip_gain.reshape(1, 32),
        write_proj,
        read_proj,
        norm_gain.reshape(1, 2048),
    )


def solution(mesh):
    tokens = P("role", "seq", "tp")
    in_specs = (
        P("role"),
        P(),
        tokens,
        tokens,
        tokens,
        tokens,
        tokens,
        tokens,
        P("tp"),
        P("tp"),
        tokens,
        tokens,
        P("tp"),
    )
    out_specs = (
        tokens,
        tokens,
        P("role", ("tp", "seq"), None, None),
        P("role", None, "seq", "tp"),
    )
    return jax.shard_map(
        on_device, mesh=mesh, in_specs=in_specs, out_specs=out_specs, check_vma=False
    )
```

```python
import jax
import jax.numpy as jnp
from jax import lax
from jax.experimental import pallas as pl
from jax.experimental.pallas import tpu as pltpu
from jax.sharding import PartitionSpec as P

MESH = pl.DeviceIdType.MESH
LOG2E = 1.4426950408889634
SCORE = 128**-0.5 * LOG2E
ROWS = 256
LANES = 128
SEQ = 16
RING = 8
HEADS = 8
STATE = 256
MSG = STATE + 16
F32 = jnp.float32
BF16 = jnp.bfloat16


def iota(shape, dim):
    return lax.broadcasted_iota(jnp.int32, shape, dim)


def kernel(
    len_ref,
    own_ref,
    q_hbm,
    k_hbm,
    v_hbm,
    x_hbm,
    g_hbm,
    st_ref,
    rate_ref,
    skip_ref,
    b_hbm,
    c_hbm,
    y_ref,
    sq_ref,
    ao_ref,
    ds_ref,
    dk_ref,
    q_ref,
    k_ref,
    v_ref,
    x_ref,
    g_ref,
    b_ref,
    c_ref,
    kvo,
    kvx,
    tx1,
    rx1,
    tx2,
    rx2,
    hkt,
    hkr,
    hst,
    hsr,
    log_ref,
    mt_ref,
    bt_ref,
    xw_ref,
    gm_ref,
    el_ref,
    sg_ref,
    qt_ref,
    sc_ref,
    wt_ref,
    top_ref,
    den_ref,
    acc_ref,
    state_ref,
    loads,
    s1,
    r1,
    s2,
    r2,
    up,
    down,
    ro,
    sx,
    rx,
    sk,
    rk,
    sf,
    rf,
):
    s, t, r = lax.axis_index("seq"), lax.axis_index("tp"), lax.axis_index("role")
    row = s // RING
    z = lax.rem(s, RING)
    across = (lax.rem(s + RING, SEQ), t, r)

    fetched = [
        pltpu.make_async_copy(src.at[0], dst, loads.at[i])
        for i, (src, dst) in enumerate(
            [
                (k_hbm, k_ref),
                (v_hbm, v_ref),
                (b_hbm, b_ref),
                (x_hbm, x_ref),
                (c_hbm, c_ref),
                (g_hbm, g_ref),
                (q_hbm, q_ref),
            ]
        )
    ]
    for copy in fetched:
        copy.start()

    def on_ring(step):
        return (row * RING + lax.rem(z + step + RING, RING), t, r)

    def owner_hop(level):
        if level == 0:
            return (s, t, 1 - r)
        width = 1 << (level - 1)
        return (s, t + width * (1 - 2 * lax.rem(t // width, 2)), r)

    def send(src, dst, ssem, rsem, device):
        return pltpu.make_async_remote_copy(
            src, dst, ssem, rsem, device_id=device, device_id_type=MESH
        )

    barrier = pltpu.get_barrier_semaphore()
    for k in range(1, SEQ):
        pl.semaphore_signal(
            barrier, inc=1, device_id=(lax.rem(s + k, SEQ), t, r), device_id_type=MESH
        )
    for level in range(4):
        pl.semaphore_signal(barrier, inc=1, device_id=owner_hop(level), device_id_type=MESH)

    def up_copy(slot):
        return send(kvo.at[slot], kvo.at[slot], up.at[slot], ro.at[slot], on_ring(1))

    def down_copy(slot):
        return send(kvo.at[slot], kvo.at[slot], down.at[slot], ro.at[slot], on_ring(-1))

    def cross_copy(slot):
        return send(kvo.at[slot], kvx.at[slot], sx.at[slot], rx.at[slot], across)

    def kv_hop(level):
        return send(
            hkt.at[level], hkr.at[level], sk.at[level], rk.at[level], owner_hop(level)
        )

    def state_hop(level):
        return send(
            hst.at[level], hsr.at[level], sf.at[level], rf.at[level], owner_hop(level)
        )

    def local_copy(pair):
        return send(tx1.at[pair], rx1.at[s], s1.at[pair], r1.at[s], (pair, t, r))

    def local_arrival(source):
        return send(tx1.at[source], rx1.at[source], s1.at[source], r1.at[source], (source, t, r))

    def prefix_copy(target):
        return send(tx2.at[target], rx2.at[s], s2.at[target], r2.at[s], (target, t, r))

    def prefix_arrival(pair):
        return send(tx2.at[pair], rx2.at[pair], s2.at[pair], r2.at[pair], (pair, t, r))

    length = len_ref[0]
    live = s * ROWS + iota((ROWS, LANES), 0) < length
    low = iota((ROWS, LANES), 1) < 64

    steps = jnp.concatenate(
        [st_ref[0].astype(F32), jnp.zeros((LANES - 32, ROWS), F32)], axis=0
    ).T
    rates = jnp.concatenate([rate_ref[...], jnp.zeros((1, LANES - 32), F32)], axis=1)
    steps = jnp.where(live, steps, 0.0)
    causal = iota((ROWS, ROWS), 0) >= iota((ROWS, ROWS), 1)
    logs = jnp.dot(
        causal.astype(F32),
        steps * rates * -LOG2E,
        precision=lax.Precision.HIGHEST,
        preferred_element_type=F32,
    )
    used = steps > 0.0
    less = jnp.where(used, logs - jnp.log(jnp.where(used, steps, 1.0)) * LOG2E, 1e9)
    log_ref[...] = logs
    weights = jnp.exp2(logs[ROWS - 1 :, :] - less)
    decays = jnp.exp2(logs[ROWS - 8 :, :])
    mt_ref[...] = less.T

    for copy in fetched[:2]:
        copy.wait()
    keys = jnp.where(live, k_ref[...].astype(F32), 0.0)
    values = jnp.where(live, v_ref[...].astype(F32), 0.0)
    flipped = values.T.astype(BF16)
    hkt[0, 0] = keys.astype(BF16)
    hkt[0, 1] = values.astype(BF16)
    kvo[z, 0] = keys.astype(BF16)
    kvo[z, 1, :LANES] = flipped[:, :LANES]
    kvo[z, 1, LANES:] = flipped[:, LANES:]
    pl.semaphore_wait(barrier, SEQ - 1 + 4)
    up_copy(z).start()
    down_copy(z).start()

    @pl.when(row == 0)
    def _():
        cross_copy(z).start()

    kv_hop(0).start()

    for copy in fetched[2:4]:
        copy.wait()
    bt_ref[...] = b_ref[...].astype(F32).T.astype(BF16)
    which = iota((16, LANES), 0)
    for pair in range(SEQ):
        cols = slice(pair * LANES, (pair + 1) * LANES)
        one, two = 2 * pair, 2 * pair + 1
        weight = jnp.where(low, weights[:, one : one + 1], weights[:, two : two + 1])
        xw_ref[:, cols] = (x_ref[:, cols].astype(F32) * weight).astype(BF16)
        decay = jnp.where(low[:1], decays[7:8, one : one + 1], decays[7:8, two : two + 1])
        high = decay.astype(BF16).astype(F32)
        middle = (decay - high).astype(BF16).astype(F32)
        rest = decay - high - middle
        tx1[pair, STATE:, :] = jnp.where(
            which == 0, high, jnp.where(which == 1, middle, jnp.where(which == 2, rest, 0.0))
        ).astype(BF16)
    for twice in range(RING):
        fresh = jnp.dot(
            bt_ref[...],
            xw_ref[:, twice * 2 * LANES : (twice + 1) * 2 * LANES],
            preferred_element_type=F32,
        ).astype(BF16)
        tx1[2 * twice, :STATE, :] = fresh[:, :LANES]
        tx1[2 * twice + 1, :STATE, :] = fresh[:, LANES:]
    for k in range(1, 5):
        local_copy(lax.rem(s + k, SEQ)).start()
    rx1[s] = tx1[s]

    fetched[4].wait()
    gm_ref[...] = jnp.where(
        causal,
        lax.dot_general(
            c_ref[...], b_ref[...], (((1,), (1,)), ((), ())), preferred_element_type=F32
        ),
        0.0,
    )
    for copy in fetched[5:]:
        copy.wait()
    key_xor = own_ref[0]
    skips = jnp.broadcast_to(
        jnp.concatenate([skip_ref[...], jnp.zeros((1, LANES - 32), F32)], axis=1), (8, LANES)
    )

    def within(four):
        shift = lax.rem(LANES - 8 * four, LANES)
        turned = pltpu.roll(log_ref[...], shift, axis=1)
        gains = pltpu.roll(skips, shift, axis=1)
        table = mt_ref[pl.ds(pl.multiple_of(8 * four, 8), 8), :]
        for j in range(4):
            cols = pl.ds(pl.multiple_of((4 * four + j) * LANES, LANES), LANES)
            heads = [2 * j, 2 * j + 1]
            columns = [jnp.broadcast_to(turned[:, i : i + 1], (ROWS, LANES)) for i in heads]
            lines = [table[i : i + 1, :] for i in heads]
            x = x_ref[:, cols].astype(F32)
            halves = [jnp.where(low, x, 0.0).astype(BF16), jnp.where(low, 0.0, x).astype(BF16)]

            def mix(head, below, right):
                rows, over = slice(below, below + 128), slice(right, right + 128)
                spread = columns[head][rows] - lines[head][:, over]
                return (gm_ref[rows, over] * jnp.exp2(spread)).astype(BF16)

            gain = jnp.where(
                low[:1], gains[:1, heads[0] : heads[0] + 1], gains[:1, heads[1] : heads[1] + 1]
            )
            skipped = gain * x
            upper = jnp.dot(
                jnp.concatenate([mix(0, 0, 0), mix(1, 0, 0)], axis=1),
                jnp.concatenate([halves[0][:128], halves[1][:128]], axis=0),
                preferred_element_type=F32,
            )
            lower = jnp.dot(
                jnp.concatenate(
                    [mix(0, 128, 0), mix(0, 128, 128), mix(1, 128, 0), mix(1, 128, 128)], axis=1
                ),
                jnp.concatenate(halves, axis=0),
                preferred_element_type=F32,
            )
            y_ref[:128, cols] = upper + skipped[:128]
            y_ref[128:, cols] = lower + skipped[128:]
            el_ref[:, cols] = jnp.exp2(jnp.where(low, columns[0], columns[1]))
            gate = g_ref[:, cols].astype(F32)
            sg_ref[:, cols] = gate / (1.0 + jnp.exp(-gate))

    def routed(level, arrived, held):
        bit = lax.rem(key_xor // (1 << (level - 1)), 2)
        take = jnp.broadcast_to(bit, arrived.shape) == 1
        return jnp.where(take, arrived.astype(F32), held.astype(F32)).astype(BF16)

    def kv_step(level):
        kv_hop(level).wait_recv()
        for part in range(2):
            moved = hkr[level, part]
            if level > 0:
                moved = routed(level, moved, hkt[level, part])
            if level < 3:
                hkt[level + 1, part] = moved
            else:
                dk_ref[0, part] = moved
        if level < 3:
            kv_hop(level + 1).start()

    def ring_turn(four, carry):
        within(four)
        for j in range(2):
            h = 2 * four + j
            cols = pl.ds(pl.multiple_of(h * LANES, LANES), LANES)
            qt_ref[h] = q_ref[:, cols].astype(F32).T.astype(BF16)
        before = lax.rem(z - four - 1 + RING, RING)
        after = lax.rem(z + four + 1, RING)
        up_copy(before).wait_recv()

        @pl.when(four < 3)
        def _():
            up_copy(before).start()
            down_copy(after).wait_recv()

        @pl.when(four < 2)
        def _():
            down_copy(after).start()

        @pl.when(four < 2)
        def _():
            for j in range(4):
                local_copy(lax.rem(s + 4 * four + 5 + j, SEQ)).start()

        @pl.when(four == 2)
        def _():
            for j in range(3):
                local_copy(lax.rem(s + 13 + j, SEQ)).start()

        @pl.when(row == 0)
        def _():
            cross_copy(before).start()

            @pl.when(four < 3)
            def _():
                cross_copy(after).start()

        for level in range(4):

            @pl.when(four == level)
            def _():
                kv_step(level)

        return carry

    lax.fori_loop(0, 4, ring_turn, 0)

    state_ref[...] = jnp.zeros((STATE, LANES), F32)

    def scan(i, carry):
        now = state_ref[...]
        tx2[i] = now.astype(BF16)

        @pl.when(i == s)
        def _():
            rx2[s] = now.astype(BF16)

        @pl.when(i != s)
        def _():
            prefix_copy(i).start()
            local_arrival(i).wait_recv()

        decay = jnp.sum(rx1[i, STATE:, :].astype(F32), axis=0, keepdims=True)
        state_ref[...] = now * decay + rx1[i, :STATE, :].astype(F32)
        return carry

    lax.fori_loop(0, SEQ, scan, 0)
    hst[0] = state_ref[...].astype(BF16)
    state_hop(0).start()

    def state_step(level):
        state_hop(level).wait_recv()
        moved = hsr[level]
        if level > 0:
            moved = routed(level, moved, hst[level])
        if level < 3:
            hst[level + 1] = moved
            state_hop(level + 1).start()
        else:
            ds_ref[0] = moved.astype(F32).T.reshape(2, 64, STATE)

    top_ref[...] = jnp.full(top_ref.shape, -1e30, F32)
    den_ref[...] = jnp.zeros(den_ref.shape, F32)
    acc_ref[...] = jnp.zeros(acc_ref.shape, F32)

    def attend(kv, first, ahead):
        def score(h):
            for w in range(4):
                sc_ref[h % 2, w * ROWS : (w + 1) * ROWS] = jnp.dot(
                    kv[first + w, 0], qt_ref[h], preferred_element_type=F32
                )

        def soften(h):
            scores = sc_ref[h % 2]
            if ahead is not None:
                apart = iota((4 * ROWS, ROWS), 0) - iota((4 * ROWS, ROWS), 1)
                scores = jnp.where(apart <= ahead, scores, -jnp.inf)
            old = top_ref[h]
            new = jnp.maximum(old, jnp.max(scores, axis=0, keepdims=True) * SCORE)
            weight = jnp.exp2(scores * SCORE - new)
            scale = jnp.exp2(old - new)
            wt_ref[h % 2] = weight.astype(BF16)
            den_ref[h] = den_ref[h] * scale + jnp.sum(weight, axis=0, keepdims=True)
            top_ref[h] = new
            return scale

        def mix(h, scale):
            part = 0.0
            for w in range(4):
                flat = kv[first + w, 1]
                part = part + jnp.dot(
                    jnp.concatenate([flat[:LANES], flat[LANES:]], axis=1),
                    wt_ref[h % 2, w * ROWS : (w + 1) * ROWS],
                    preferred_element_type=F32,
                )
            acc_ref[h] = acc_ref[h] * scale + part

        score(0)
        for h in range(HEADS):
            if h + 1 < HEADS:
                score(h + 1)
            mix(h, soften(h))

    def own_row(part, carry):
        @pl.when(z >= 4 * part)
        def _():
            attend(kvo, 4 * part, z * ROWS - part * 4 * ROWS)

        for level in range(2):

            @pl.when(part == level)
            def _():
                state_step(level)

        return carry

    lax.fori_loop(0, 2, own_row, 0)

    def other_row(part, carry):
        @pl.when(row == 1)
        def _():
            for w in range(4):
                cross_copy(4 * part + w).wait_recv()
            attend(kvx, 4 * part, None)

        for level in range(2):

            @pl.when(part == level)
            def _():
                state_step(level + 2)

        return carry

    lax.fori_loop(0, 2, other_row, 0)

    for h in range(HEADS):
        attended = (acc_ref[h] / den_ref[h]).T
        ao_ref[0, :, h * LANES : (h + 1) * LANES] = jnp.where(live, attended, 0.0).astype(BF16)

    sq_ref[...] = jnp.zeros((ROWS, LANES), F32)

    def outputs(twice, carry):
        pairs = [lax.rem(s + 2 * twice + j, SEQ) for j in range(2)]
        for j, pair in enumerate(pairs):
            if j == 0:

                @pl.when(twice > 0)
                def _():
                    prefix_arrival(pair).wait_recv()

            else:
                prefix_arrival(pair).wait_recv()
        carried = jnp.dot(
            c_ref[...],
            jnp.concatenate([rx2[pair] for pair in pairs], axis=1),
            preferred_element_type=F32,
        )
        for j, pair in enumerate(pairs):
            cols = pl.ds(pl.multiple_of(pair * LANES, LANES), LANES)
            mine = carried[:, j * LANES : (j + 1) * LANES]
            mixed = (y_ref[:, cols] + el_ref[:, cols] * mine).astype(BF16).astype(F32)
            gated = mixed * sg_ref[:, cols]
            y_ref[:, cols] = gated
            sq_ref[...] += gated * gated
        return carry

    lax.fori_loop(0, RING, outputs, 0)
    mean = jnp.sum(sq_ref[...], axis=1, keepdims=True) * (1.0 / 2048.0)
    sq_ref[...] = jnp.where(live, lax.rsqrt(mean + 1e-05), 0.0)

    for k in range(1, SEQ):
        local_copy(lax.rem(s + k, SEQ)).wait_send()
        prefix_copy(lax.rem(s + k, SEQ)).wait_send()
    for k in range(4):
        up_copy(lax.rem(z - k + RING, RING)).wait_send()
    for k in range(3):
        down_copy(lax.rem(z + k, RING)).wait_send()

    @pl.when(row == 0)
    def _():
        for slot in range(RING):
            cross_copy(slot).wait_send()

    for level in range(4):
        kv_hop(level).wait_send()
        state_hop(level).wait_send()


def finish(y_ref, factor_ref, gain_ref, ao_in, ds_in, dk_in, mo_ref, ao_ref, ds_ref, dk_ref):
    for i in range(y_ref.shape[1] // LANES):
        cols = slice(i * LANES, (i + 1) * LANES)
        mo_ref[0, :, cols] = (y_ref[:, cols] * factor_ref[...] * gain_ref[:, cols]).astype(BF16)
    ao_ref[...] = ao_in[...]
    ds_ref[...] = ds_in[...]
    dk_ref[...] = dk_in[...]


def on_device(
    prompt_length,
    owner_map,
    queries,
    key_rows,
    value_matrix,
    ssm_input,
    gate_input,
    step_sizes,
    decay_rate,
    skip_gain,
    write_proj,
    read_proj,
    norm_gain,
):
    smem = pl.BlockSpec(memory_space=pltpu.SMEM)
    vmem = pl.BlockSpec(memory_space=pltpu.VMEM)
    hbm = pl.BlockSpec(memory_space=pltpu.HBM)
    dma = pltpu.SemaphoreType.DMA
    wide = pltpu.VMEM((ROWS, SEQ * LANES), F32)
    tokens = pltpu.VMEM((ROWS, SEQ * LANES), BF16)
    square = pltpu.VMEM((ROWS, LANES), F32)
    narrow = pltpu.VMEM((ROWS, LANES), BF16)
    group = pltpu.VMEM((ROWS, STATE), BF16)
    block = pltpu.VMEM((RING, 2, ROWS, LANES), BF16)
    gated, factor, attn, state, kv = pl.pallas_call(
        kernel,
        name="prefill",
        out_shape=(
            jax.ShapeDtypeStruct((ROWS, 2048), F32),
            jax.ShapeDtypeStruct((ROWS, LANES), F32),
            jax.ShapeDtypeStruct((1, ROWS, 1024), BF16),
            jax.ShapeDtypeStruct((1, 2, 64, STATE), F32),
            jax.ShapeDtypeStruct((1, 2, ROWS, LANES), BF16),
        ),
        in_specs=[smem, smem, hbm, hbm, hbm, hbm, hbm, vmem, vmem, vmem, hbm, hbm],
        out_specs=(vmem,) * 5,
        scratch_shapes=[
            pltpu.VMEM((ROWS, 1024), BF16),
            narrow,
            narrow,
            tokens,
            tokens,
            group,
            group,
            block,
            block,
            pltpu.VMEM((SEQ, MSG, LANES), BF16),
            pltpu.VMEM((SEQ, MSG, LANES), BF16),
            pltpu.VMEM((SEQ, STATE, LANES), BF16),
            pltpu.VMEM((SEQ, STATE, LANES), BF16),
            pltpu.VMEM((4, 2, ROWS, LANES), BF16),
            pltpu.VMEM((4, 2, ROWS, LANES), BF16),
            pltpu.VMEM((4, STATE, LANES), BF16),
            pltpu.VMEM((4, STATE, LANES), BF16),
            square,
            pltpu.VMEM((LANES, ROWS), F32),
            group,
            tokens,
            pltpu.VMEM((ROWS, ROWS), F32),
            wide,
            wide,
            pltpu.VMEM((HEADS, LANES, ROWS), BF16),
            pltpu.VMEM((2, 4 * ROWS, ROWS), F32),
            pltpu.VMEM((2, 4 * ROWS, ROWS), BF16),
            pltpu.VMEM((HEADS, 1, ROWS), F32),
            pltpu.VMEM((HEADS, 1, ROWS), F32),
            pltpu.VMEM((HEADS, LANES, ROWS), F32),
            pltpu.VMEM((STATE, LANES), F32),
            dma((7,)),
            dma((SEQ,)),
            dma((SEQ,)),
            dma((SEQ,)),
            dma((SEQ,)),
            dma((RING,)),
            dma((RING,)),
            dma((RING,)),
            dma((RING,)),
            dma((RING,)),
            dma((4,)),
            dma((4,)),
            dma((4,)),
            dma((4,)),
        ],
        compiler_params=pltpu.CompilerParams(
            collective_id=0, has_side_effects=True, vmem_limit_bytes=63 * 2**20
        ),
    )(
        prompt_length,
        owner_map,
        queries,
        key_rows,
        value_matrix,
        ssm_input,
        gate_input,
        jnp.swapaxes(step_sizes, 1, 2),
        decay_rate.reshape(1, 32),
        skip_gain.reshape(1, 32),
        write_proj,
        read_proj,
    )
    part = 512
    passed = [
        pl.BlockSpec((1, ROWS, 256), lambda i: (0, 0, i)),
        pl.BlockSpec((1, 2, 16, STATE), lambda i: (0, 0, i, 0)),
        pl.BlockSpec((1, 2, 64, LANES), lambda i: (0, 0, i, 0)),
    ]
    return pl.pallas_call(
        finish,
        name="finish",
        grid=(2048 // part,),
        out_shape=(
            jax.ShapeDtypeStruct((1, ROWS, 2048), BF16),
            jax.ShapeDtypeStruct(attn.shape, attn.dtype),
            jax.ShapeDtypeStruct(state.shape, state.dtype),
            jax.ShapeDtypeStruct(kv.shape, kv.dtype),
        ),
        in_specs=[
            pl.BlockSpec((ROWS, part), lambda i: (0, i)),
            pl.BlockSpec((ROWS, LANES), lambda i: (0, 0)),
            pl.BlockSpec((1, part), lambda i: (0, i)),
            *passed,
        ],
        out_specs=(pl.BlockSpec((1, ROWS, part), lambda i: (0, 0, i)), *passed),
    )(gated, factor, norm_gain.reshape(1, 2048), attn, state, kv)


def solution(mesh):
    tokens = P("role", "seq", "tp")
    in_specs = (
        P("role"),
        P(),
        tokens,
        tokens,
        tokens,
        tokens,
        tokens,
        tokens,
        P("tp"),
        P("tp"),
        tokens,
        tokens,
        P("tp"),
    )
    out_specs = (
        tokens,
        tokens,
        P("role", ("tp", "seq"), None, None),
        P("role", None, "seq", "tp"),
    )
    return jax.shard_map(
        on_device, mesh=mesh, in_specs=in_specs, out_specs=out_specs, check_vma=False
    )
```

```python
import jax
import jax.numpy as jnp
from jax import lax
from jax.experimental import pallas as pl
from jax.experimental.pallas import tpu as pltpu
from jax.sharding import PartitionSpec as P

MESH = pl.DeviceIdType.MESH
LOG2E = 1.4426950408889634
SCORE = 128**-0.5 * LOG2E
ROWS = 256
LANES = 128
SEQ = 16
RING = 8
HEADS = 8
STATE = 256
HEAD = 16
HALF = STATE // 2
F32 = jnp.float32
BF16 = jnp.bfloat16


def iota(shape, dim):
    return lax.broadcasted_iota(jnp.int32, shape, dim)


def kernel(
    len_ref,
    own_ref,
    q_hbm,
    k_hbm,
    v_hbm,
    x_hbm,
    g_hbm,
    st_ref,
    rate_ref,
    skip_ref,
    b_hbm,
    c_hbm,
    y_ref,
    sq_ref,
    ao_ref,
    ds_ref,
    dk_ref,
    q_ref,
    k_ref,
    v_ref,
    x_ref,
    g_ref,
    b_ref,
    c_ref,
    kvo,
    kvx,
    tx1,
    rx1,
    tx2,
    rx2,
    hkt,
    hkr,
    hst,
    hsr,
    log_ref,
    mt_ref,
    bt_ref,
    xw_ref,
    gm_ref,
    el_ref,
    sg_ref,
    qt_ref,
    sc_ref,
    wt_ref,
    top_ref,
    den_ref,
    acc_ref,
    state_ref,
    loads,
    s1,
    r1,
    s2,
    r2,
    up,
    down,
    ro,
    sx,
    rx,
    sk,
    rk,
    sf,
    rf,
):
    s, t, r = lax.axis_index("seq"), lax.axis_index("tp"), lax.axis_index("role")
    row = s // RING
    z = lax.rem(s, RING)
    across = (lax.rem(s + RING, SEQ), t, r)

    fetched = [
        pltpu.make_async_copy(src.at[0], dst, loads.at[i])
        for i, (src, dst) in enumerate(
            [
                (k_hbm, k_ref),
                (v_hbm, v_ref),
                (b_hbm, b_ref),
                (x_hbm, x_ref),
                (c_hbm, c_ref),
                (g_hbm, g_ref),
                (q_hbm, q_ref),
            ]
        )
    ]
    for copy in fetched:
        copy.start()

    def on_ring(step):
        return (row * RING + lax.rem(z + step + RING, RING), t, r)

    def owner_hop(level):
        if level == 0:
            return (s, t, 1 - r)
        width = 1 << (level - 1)
        return (s, t + width * (1 - 2 * lax.rem(t // width, 2)), r)

    def send(src, dst, ssem, rsem, device):
        return pltpu.make_async_remote_copy(
            src, dst, ssem, rsem, device_id=device, device_id_type=MESH
        )

    barrier = pltpu.get_barrier_semaphore()
    for k in range(1, SEQ):
        pl.semaphore_signal(
            barrier, inc=1, device_id=(lax.rem(s + k, SEQ), t, r), device_id_type=MESH
        )
    for level in range(4):
        pl.semaphore_signal(barrier, inc=1, device_id=owner_hop(level), device_id_type=MESH)

    def up_copy(slot):
        return send(kvo.at[slot], kvo.at[slot], up.at[slot], ro.at[slot], on_ring(1))

    def down_copy(slot):
        return send(kvo.at[slot], kvo.at[slot], down.at[slot], ro.at[slot], on_ring(-1))

    def cross_copy(slot):
        return send(kvo.at[slot], kvx.at[slot], sx.at[slot], rx.at[slot], across)

    def kv_hop(level):
        return send(
            hkt.at[level], hkr.at[level], sk.at[level], rk.at[level], owner_hop(level)
        )

    def state_hop(level):
        return send(
            hst.at[level], hsr.at[level], sf.at[level], rf.at[level], owner_hop(level)
        )

    def part_rows(part, first):
        return pl.ds(first + part * HALF, HALF) if part else pl.ds(0, first + HALF)

    def local_send(here, there, part, device):
        rows = part_rows(part, HEAD)
        return send(
            tx1.at[here, rows],
            rx1.at[there, rows],
            s1.at[part * SEQ + here],
            r1.at[part * SEQ + there],
            (device, t, r),
        )

    def prefix_send(here, there, part, device):
        rows = part_rows(part, 0)
        return send(
            tx2.at[here, rows],
            rx2.at[there, rows],
            s2.at[part * SEQ + here],
            r2.at[part * SEQ + there],
            (device, t, r),
        )

    def local_copy(pair, part):
        return local_send(pair, s, part, pair)

    def local_arrival(source, part):
        return local_send(source, source, part, source)

    def prefix_copy(target, part):
        return prefix_send(target, s, part, target)

    def prefix_arrival(pair, part):
        return prefix_send(pair, pair, part, pair)

    length = len_ref[0]
    live = s * ROWS + iota((ROWS, LANES), 0) < length
    low = iota((ROWS, LANES), 1) < 64

    steps = jnp.concatenate(
        [st_ref[0].astype(F32), jnp.zeros((LANES - 32, ROWS), F32)], axis=0
    ).T
    rates = jnp.concatenate([rate_ref[...], jnp.zeros((1, LANES - 32), F32)], axis=1)
    steps = jnp.where(live, steps, 0.0)
    causal = iota((ROWS, ROWS), 0) >= iota((ROWS, ROWS), 1)
    logs = jnp.dot(
        causal.astype(F32),
        steps * rates * -LOG2E,
        precision=lax.Precision.HIGHEST,
        preferred_element_type=F32,
    )
    used = steps > 0.0
    less = jnp.where(used, logs - jnp.log(jnp.where(used, steps, 1.0)) * LOG2E, 1e9)
    log_ref[...] = logs
    weights = jnp.exp2(logs[ROWS - 1 :, :] - less)
    decays = jnp.exp2(logs[ROWS - 8 :, :])
    mt_ref[...] = less.T

    for copy in fetched[:2]:
        copy.wait()
    keys = jnp.where(live, k_ref[...].astype(F32), 0.0)
    values = jnp.where(live, v_ref[...].astype(F32), 0.0)
    flipped = values.T.astype(BF16)
    hkt[0, 0] = keys.astype(BF16)
    hkt[0, 1] = values.astype(BF16)
    kvo[z, 0] = keys.astype(BF16)
    kvo[z, 1, :LANES] = flipped[:, :LANES]
    kvo[z, 1, LANES:] = flipped[:, LANES:]
    pl.semaphore_wait(barrier, SEQ - 1 + 4)
    up_copy(z).start()
    down_copy(z).start()

    @pl.when(row == 0)
    def _():
        cross_copy(z).start()

    kv_hop(0).start()

    for copy in fetched[2:4]:
        copy.wait()
    bt_ref[...] = b_ref[...].astype(F32).T.astype(BF16)
    which = iota((16, LANES), 0)
    for pair in range(SEQ):
        cols = slice(pair * LANES, (pair + 1) * LANES)
        one, two = 2 * pair, 2 * pair + 1
        weight = jnp.where(low, weights[:, one : one + 1], weights[:, two : two + 1])
        xw_ref[:, cols] = (x_ref[:, cols].astype(F32) * weight).astype(BF16)
        decay = jnp.where(low[:1], decays[7:8, one : one + 1], decays[7:8, two : two + 1])
        high = decay.astype(BF16).astype(F32)
        middle = (decay - high).astype(BF16).astype(F32)
        rest = decay - high - middle
        tx1[pair, :HEAD, :] = jnp.where(
            which == 0, high, jnp.where(which == 1, middle, jnp.where(which == 2, rest, 0.0))
        ).astype(BF16)
    for twice in range(RING):
        fresh = jnp.dot(
            bt_ref[...],
            xw_ref[:, twice * 2 * LANES : (twice + 1) * 2 * LANES],
            preferred_element_type=F32,
        ).astype(BF16)
        tx1[2 * twice, HEAD:, :] = fresh[:, :LANES]
        tx1[2 * twice + 1, HEAD:, :] = fresh[:, LANES:]
    groups = [(0, 1, 9), (0, 9, SEQ), (1, 1, 9), (1, 9, SEQ)]

    def send_group(index):
        part, first, end = groups[index]
        for k in range(first, end):
            local_copy(lax.rem(s + k, SEQ), part).start()

    send_group(0)
    rx1[s] = tx1[s]

    fetched[4].wait()
    gm_ref[...] = jnp.where(
        causal,
        lax.dot_general(
            c_ref[...], b_ref[...], (((1,), (1,)), ((), ())), preferred_element_type=F32
        ),
        0.0,
    )
    for copy in fetched[5:]:
        copy.wait()
    key_xor = own_ref[0]
    skips = jnp.broadcast_to(
        jnp.concatenate([skip_ref[...], jnp.zeros((1, LANES - 32), F32)], axis=1), (8, LANES)
    )

    def within(four):
        shift = lax.rem(LANES - 8 * four, LANES)
        turned = pltpu.roll(log_ref[...], shift, axis=1)
        gains = pltpu.roll(skips, shift, axis=1)
        table = mt_ref[pl.ds(pl.multiple_of(8 * four, 8), 8), :]
        for j in range(4):
            cols = pl.ds(pl.multiple_of((4 * four + j) * LANES, LANES), LANES)
            heads = [2 * j, 2 * j + 1]
            columns = [jnp.broadcast_to(turned[:, i : i + 1], (ROWS, LANES)) for i in heads]
            lines = [table[i : i + 1, :] for i in heads]
            x = x_ref[:, cols].astype(F32)
            halves = [jnp.where(low, x, 0.0).astype(BF16), jnp.where(low, 0.0, x).astype(BF16)]

            def mix(head, below, right):
                rows, over = slice(below, below + 128), slice(right, right + 128)
                spread = columns[head][rows] - lines[head][:, over]
                return (gm_ref[rows, over] * jnp.exp2(spread)).astype(BF16)

            gain = jnp.where(
                low[:1], gains[:1, heads[0] : heads[0] + 1], gains[:1, heads[1] : heads[1] + 1]
            )
            skipped = gain * x
            upper = jnp.dot(
                jnp.concatenate([mix(0, 0, 0), mix(1, 0, 0)], axis=1),
                jnp.concatenate([halves[0][:128], halves[1][:128]], axis=0),
                preferred_element_type=F32,
            )
            lower = jnp.dot(
                jnp.concatenate(
                    [mix(0, 128, 0), mix(0, 128, 128), mix(1, 128, 0), mix(1, 128, 128)], axis=1
                ),
                jnp.concatenate(halves, axis=0),
                preferred_element_type=F32,
            )
            y_ref[:128, cols] = upper + skipped[:128]
            y_ref[128:, cols] = lower + skipped[128:]
            el_ref[:, cols] = jnp.exp2(jnp.where(low, columns[0], columns[1]))
            gate = g_ref[:, cols].astype(F32)
            sg_ref[:, cols] = gate / (1.0 + jnp.exp(-gate))

    def routed(level, arrived, held):
        bit = lax.rem(key_xor // (1 << (level - 1)), 2)
        take = jnp.broadcast_to(bit, arrived.shape) == 1
        return jnp.where(take, arrived.astype(F32), held.astype(F32)).astype(BF16)

    def kv_step(level):
        kv_hop(level).wait_recv()
        for part in range(2):
            moved = hkr[level, part]
            if level > 0:
                moved = routed(level, moved, hkt[level, part])
            if level < 3:
                hkt[level + 1, part] = moved
            else:
                dk_ref[0, part] = moved
        if level < 3:
            kv_hop(level + 1).start()

    def ring_turn(four, carry):
        within(four)
        for j in range(2):
            h = 2 * four + j
            cols = pl.ds(pl.multiple_of(h * LANES, LANES), LANES)
            qt_ref[h] = q_ref[:, cols].astype(F32).T.astype(BF16)
        before = lax.rem(z - four - 1 + RING, RING)
        after = lax.rem(z + four + 1, RING)
        up_copy(before).wait_recv()

        @pl.when(four < 3)
        def _():
            up_copy(before).start()
            down_copy(after).wait_recv()

        @pl.when(four < 2)
        def _():
            down_copy(after).start()

        for index in range(1, 4):

            @pl.when(four == index - 1)
            def _():
                send_group(index)

        @pl.when(row == 0)
        def _():
            cross_copy(before).start()

            @pl.when(four < 3)
            def _():
                cross_copy(after).start()

        for level in range(4):

            @pl.when(four == level)
            def _():
                kv_step(level)

        return carry

    lax.fori_loop(0, 4, ring_turn, 0)

    state_ref[...] = jnp.zeros((STATE, LANES), F32)

    def scan(part):
        rows = slice(part * HALF, (part + 1) * HALF)
        stored = slice(HEAD + part * HALF, HEAD + (part + 1) * HALF)

        def turn(i, carry):
            now = state_ref[rows]
            tx2[i, rows] = now.astype(BF16)

            @pl.when(i == s)
            def _():
                rx2[s, rows] = now.astype(BF16)

            @pl.when(i != s)
            def _():
                prefix_copy(i, part).start()
                local_arrival(i, part).wait_recv()

            decay = jnp.sum(rx1[i, :HEAD, :].astype(F32), axis=0, keepdims=True)
            state_ref[rows] = now * decay + rx1[i, stored, :].astype(F32)
            return carry

        lax.fori_loop(0, SEQ, turn, 0)

    scan(0)
    scan(1)
    hst[0] = state_ref[...].astype(BF16)
    state_hop(0).start()

    def state_step(level):
        state_hop(level).wait_recv()
        moved = hsr[level]
        if level > 0:
            moved = routed(level, moved, hst[level])
        if level < 3:
            hst[level + 1] = moved
            state_hop(level + 1).start()
        else:
            ds_ref[0] = moved.astype(F32).T.reshape(2, 64, STATE)

    top_ref[...] = jnp.full(top_ref.shape, -1e30, F32)
    den_ref[...] = jnp.zeros(den_ref.shape, F32)
    acc_ref[...] = jnp.zeros(acc_ref.shape, F32)

    def attend(kv, first, ahead):
        def score(h):
            for w in range(4):
                sc_ref[h % 2, w * ROWS : (w + 1) * ROWS] = jnp.dot(
                    kv[first + w, 0], qt_ref[h], preferred_element_type=F32
                )

        def soften(h):
            scores = sc_ref[h % 2]
            if ahead is not None:
                apart = iota((4 * ROWS, ROWS), 0) - iota((4 * ROWS, ROWS), 1)
                scores = jnp.where(apart <= ahead, scores, -jnp.inf)
            old = top_ref[h]
            new = jnp.maximum(old, jnp.max(scores, axis=0, keepdims=True) * SCORE)
            weight = jnp.exp2(scores * SCORE - new)
            scale = jnp.exp2(old - new)
            wt_ref[h % 2] = weight.astype(BF16)
            den_ref[h] = den_ref[h] * scale + jnp.sum(weight, axis=0, keepdims=True)
            top_ref[h] = new
            return scale

        def mix(h, scale):
            part = 0.0
            for w in range(4):
                flat = kv[first + w, 1]
                part = part + jnp.dot(
                    jnp.concatenate([flat[:LANES], flat[LANES:]], axis=1),
                    wt_ref[h % 2, w * ROWS : (w + 1) * ROWS],
                    preferred_element_type=F32,
                )
            acc_ref[h] = acc_ref[h] * scale + part

        score(0)
        for h in range(HEADS):
            if h + 1 < HEADS:
                score(h + 1)
            mix(h, soften(h))

    def own_row(part, carry):
        @pl.when(z >= 4 * part)
        def _():
            attend(kvo, 4 * part, z * ROWS - part * 4 * ROWS)

        for level in range(2):

            @pl.when(part == level)
            def _():
                state_step(level)

        return carry

    lax.fori_loop(0, 2, own_row, 0)

    def other_row(part, carry):
        @pl.when(row == 1)
        def _():
            for w in range(4):
                cross_copy(4 * part + w).wait_recv()
            attend(kvx, 4 * part, None)

        for level in range(2):

            @pl.when(part == level)
            def _():
                state_step(level + 2)

        return carry

    lax.fori_loop(0, 2, other_row, 0)

    for h in range(HEADS):
        attended = (acc_ref[h] / den_ref[h]).T
        ao_ref[0, :, h * LANES : (h + 1) * LANES] = jnp.where(live, attended, 0.0).astype(BF16)

    sq_ref[...] = jnp.zeros((ROWS, LANES), F32)

    def outputs(part):
        rows = slice(part * HALF, (part + 1) * HALF)

        def turn(twice, carry):
            pairs = [lax.rem(s + 2 * twice + j, SEQ) for j in range(2)]

            @pl.when(twice > 0)
            def _():
                prefix_arrival(pairs[0], part).wait_recv()

            prefix_arrival(pairs[1], part).wait_recv()
            carried = jnp.dot(
                c_ref[:, rows],
                jnp.concatenate([rx2[pair, rows] for pair in pairs], axis=1),
                preferred_element_type=F32,
            )
            for j, pair in enumerate(pairs):
                cols = pl.ds(pl.multiple_of(pair * LANES, LANES), LANES)
                mine = carried[:, j * LANES : (j + 1) * LANES]
                total = y_ref[:, cols] + el_ref[:, cols] * mine
                if part == 0:
                    y_ref[:, cols] = total
                else:
                    gated = total.astype(BF16).astype(F32) * sg_ref[:, cols]
                    y_ref[:, cols] = gated
                    sq_ref[...] += gated * gated
            return carry

        lax.fori_loop(0, RING, turn, 0)

    outputs(0)
    outputs(1)
    mean = jnp.sum(sq_ref[...], axis=1, keepdims=True) * (1.0 / 2048.0)
    sq_ref[...] = jnp.where(live, lax.rsqrt(mean + 1e-05), 0.0)

    for k in range(1, SEQ):
        for part in range(2):
            local_copy(lax.rem(s + k, SEQ), part).wait_send()
            prefix_copy(lax.rem(s + k, SEQ), part).wait_send()
    for k in range(4):
        up_copy(lax.rem(z - k + RING, RING)).wait_send()
    for k in range(3):
        down_copy(lax.rem(z + k, RING)).wait_send()

    @pl.when(row == 0)
    def _():
        for slot in range(RING):
            cross_copy(slot).wait_send()

    for level in range(4):
        kv_hop(level).wait_send()
        state_hop(level).wait_send()


def finish(y_ref, factor_ref, gain_ref, ao_in, ds_in, dk_in, mo_ref, ao_ref, ds_ref, dk_ref):
    for i in range(y_ref.shape[1] // LANES):
        cols = slice(i * LANES, (i + 1) * LANES)
        mo_ref[0, :, cols] = (y_ref[:, cols] * factor_ref[...] * gain_ref[:, cols]).astype(BF16)
    ao_ref[...] = ao_in[...]
    ds_ref[...] = ds_in[...]
    dk_ref[...] = dk_in[...]


def on_device(
    prompt_length,
    owner_map,
    queries,
    key_rows,
    value_matrix,
    ssm_input,
    gate_input,
    step_sizes,
    decay_rate,
    skip_gain,
    write_proj,
    read_proj,
    norm_gain,
):
    smem = pl.BlockSpec(memory_space=pltpu.SMEM)
    vmem = pl.BlockSpec(memory_space=pltpu.VMEM)
    hbm = pl.BlockSpec(memory_space=pltpu.HBM)
    dma = pltpu.SemaphoreType.DMA
    wide = pltpu.VMEM((ROWS, SEQ * LANES), F32)
    tokens = pltpu.VMEM((ROWS, SEQ * LANES), BF16)
    square = pltpu.VMEM((ROWS, LANES), F32)
    narrow = pltpu.VMEM((ROWS, LANES), BF16)
    group = pltpu.VMEM((ROWS, STATE), BF16)
    block = pltpu.VMEM((RING, 2, ROWS, LANES), BF16)
    gated, factor, attn, state, kv = pl.pallas_call(
        kernel,
        name="prefill",
        out_shape=(
            jax.ShapeDtypeStruct((ROWS, 2048), F32),
            jax.ShapeDtypeStruct((ROWS, LANES), F32),
            jax.ShapeDtypeStruct((1, ROWS, 1024), BF16),
            jax.ShapeDtypeStruct((1, 2, 64, STATE), F32),
            jax.ShapeDtypeStruct((1, 2, ROWS, LANES), BF16),
        ),
        in_specs=[smem, smem, hbm, hbm, hbm, hbm, hbm, vmem, vmem, vmem, hbm, hbm],
        out_specs=(vmem,) * 5,
        scratch_shapes=[
            pltpu.VMEM((ROWS, 1024), BF16),
            narrow,
            narrow,
            tokens,
            tokens,
            group,
            group,
            block,
            block,
            pltpu.VMEM((SEQ, HEAD + STATE, LANES), BF16),
            pltpu.VMEM((SEQ, HEAD + STATE, LANES), BF16),
            pltpu.VMEM((SEQ, STATE, LANES), BF16),
            pltpu.VMEM((SEQ, STATE, LANES), BF16),
            pltpu.VMEM((4, 2, ROWS, LANES), BF16),
            pltpu.VMEM((4, 2, ROWS, LANES), BF16),
            pltpu.VMEM((4, STATE, LANES), BF16),
            pltpu.VMEM((4, STATE, LANES), BF16),
            square,
            pltpu.VMEM((LANES, ROWS), F32),
            group,
            tokens,
            pltpu.VMEM((ROWS, ROWS), F32),
            wide,
            wide,
            pltpu.VMEM((HEADS, LANES, ROWS), BF16),
            pltpu.VMEM((2, 4 * ROWS, ROWS), F32),
            pltpu.VMEM((2, 4 * ROWS, ROWS), BF16),
            pltpu.VMEM((HEADS, 1, ROWS), F32),
            pltpu.VMEM((HEADS, 1, ROWS), F32),
            pltpu.VMEM((HEADS, LANES, ROWS), F32),
            pltpu.VMEM((STATE, LANES), F32),
            dma((7,)),
            dma((2 * SEQ,)),
            dma((2 * SEQ,)),
            dma((2 * SEQ,)),
            dma((2 * SEQ,)),
            dma((RING,)),
            dma((RING,)),
            dma((RING,)),
            dma((RING,)),
            dma((RING,)),
            dma((4,)),
            dma((4,)),
            dma((4,)),
            dma((4,)),
        ],
        compiler_params=pltpu.CompilerParams(
            collective_id=0, has_side_effects=True, vmem_limit_bytes=63 * 2**20
        ),
    )(
        prompt_length,
        owner_map,
        queries,
        key_rows,
        value_matrix,
        ssm_input,
        gate_input,
        jnp.swapaxes(step_sizes, 1, 2),
        decay_rate.reshape(1, 32),
        skip_gain.reshape(1, 32),
        write_proj,
        read_proj,
    )
    part = 1024
    passed = [
        pl.BlockSpec((1, ROWS, 512), lambda i: (0, 0, i)),
        pl.BlockSpec((1, 2, 32, STATE), lambda i: (0, 0, i, 0)),
        pl.BlockSpec((1, 2, 128, LANES), lambda i: (0, 0, i, 0)),
    ]
    return pl.pallas_call(
        finish,
        name="finish",
        grid=(2048 // part,),
        out_shape=(
            jax.ShapeDtypeStruct((1, ROWS, 2048), BF16),
            jax.ShapeDtypeStruct(attn.shape, attn.dtype),
            jax.ShapeDtypeStruct(state.shape, state.dtype),
            jax.ShapeDtypeStruct(kv.shape, kv.dtype),
        ),
        in_specs=[
            pl.BlockSpec((ROWS, part), lambda i: (0, i)),
            pl.BlockSpec((ROWS, LANES), lambda i: (0, 0)),
            pl.BlockSpec((1, part), lambda i: (0, i)),
            *passed,
        ],
        out_specs=(pl.BlockSpec((1, ROWS, part), lambda i: (0, 0, i)), *passed),
    )(gated, factor, norm_gain.reshape(1, 2048), attn, state, kv)


def solution(mesh):
    tokens = P("role", "seq", "tp")
    in_specs = (
        P("role"),
        P(),
        tokens,
        tokens,
        tokens,
        tokens,
        tokens,
        tokens,
        P("tp"),
        P("tp"),
        tokens,
        tokens,
        P("tp"),
    )
    out_specs = (
        tokens,
        tokens,
        P("role", ("tp", "seq"), None, None),
        P("role", None, "seq", "tp"),
    )
    return jax.shard_map(
        on_device, mesh=mesh, in_specs=in_specs, out_specs=out_specs, check_vma=False
    )
```

```python
import jax
import jax.numpy as jnp
from jax import lax
from jax.experimental import pallas as pl
from jax.experimental.pallas import tpu as pltpu
from jax.sharding import PartitionSpec as P

MESH = pl.DeviceIdType.MESH
LOG2E = 1.4426950408889634
SCORE = 128**-0.5 * LOG2E
ROWS = 256
LANES = 128
SEQ = 16
RING = 8
HEADS = 8
STATE = 256
HEAD = 16
HALF = STATE // 2
F32 = jnp.float32
BF16 = jnp.bfloat16


def iota(shape, dim):
    return lax.broadcasted_iota(jnp.int32, shape, dim)


def kernel(
    len_ref,
    own_ref,
    q_hbm,
    k_hbm,
    v_hbm,
    x_hbm,
    g_hbm,
    st_ref,
    rate_ref,
    skip_ref,
    b_hbm,
    c_hbm,
    y_ref,
    sq_ref,
    ao_ref,
    ds_ref,
    dk_ref,
    q_ref,
    k_ref,
    v_ref,
    x_ref,
    g_ref,
    b_ref,
    c_ref,
    kvo,
    kvx,
    tx1,
    rx1,
    tx2,
    rx2,
    hkt,
    hkr,
    hst,
    hsr,
    log_ref,
    mt_ref,
    bt_ref,
    xw_ref,
    gm_ref,
    el_ref,
    sg_ref,
    qt_ref,
    sc_ref,
    wt_ref,
    top_ref,
    den_ref,
    acc_ref,
    state_ref,
    loads,
    s1,
    r1,
    s2,
    r2,
    up,
    down,
    ro,
    sx,
    rx,
    sk,
    rk,
    sf,
    rf,
):
    s, t, r = lax.axis_index("seq"), lax.axis_index("tp"), lax.axis_index("role")
    row = s // RING
    z = lax.rem(s, RING)
    across = (lax.rem(s + RING, SEQ), t, r)

    fetched = [
        pltpu.make_async_copy(src.at[0], dst, loads.at[i])
        for i, (src, dst) in enumerate(
            [
                (k_hbm, k_ref),
                (v_hbm, v_ref),
                (b_hbm, b_ref),
                (x_hbm, x_ref),
                (c_hbm, c_ref),
                (g_hbm, g_ref),
                (q_hbm, q_ref),
            ]
        )
    ]
    for copy in fetched:
        copy.start()

    def on_ring(step):
        return (row * RING + lax.rem(z + step + RING, RING), t, r)

    def owner_hop(level):
        if level == 0:
            return (s, t, 1 - r)
        width = 1 << (level - 1)
        return (s, t + width * (1 - 2 * lax.rem(t // width, 2)), r)

    def send(src, dst, ssem, rsem, device):
        return pltpu.make_async_remote_copy(
            src, dst, ssem, rsem, device_id=device, device_id_type=MESH
        )

    barrier = pltpu.get_barrier_semaphore()
    for k in range(1, SEQ):
        pl.semaphore_signal(
            barrier, inc=1, device_id=(lax.rem(s + k, SEQ), t, r), device_id_type=MESH
        )
    for level in range(4):
        pl.semaphore_signal(barrier, inc=1, device_id=owner_hop(level), device_id_type=MESH)

    def up_copy(slot):
        return send(kvo.at[slot], kvo.at[slot], up.at[slot], ro.at[slot], on_ring(1))

    def down_copy(slot):
        return send(kvo.at[slot], kvo.at[slot], down.at[slot], ro.at[slot], on_ring(-1))

    def cross_copy(slot):
        return send(kvo.at[slot], kvx.at[slot], sx.at[slot], rx.at[slot], across)

    def kv_hop(level):
        return send(
            hkt.at[level], hkr.at[level], sk.at[level], rk.at[level], owner_hop(level)
        )

    def state_hop(level):
        return send(
            hst.at[level], hsr.at[level], sf.at[level], rf.at[level], owner_hop(level)
        )

    def part_rows(part, first):
        return pl.ds(first + part * HALF, HALF) if part else pl.ds(0, first + HALF)

    def local_send(here, there, part, device):
        rows = part_rows(part, HEAD)
        return send(
            tx1.at[here, rows],
            rx1.at[there, rows],
            s1.at[part * SEQ + here],
            r1.at[part * SEQ + there],
            (device, t, r),
        )

    def prefix_send(here, there, part, device):
        rows = part_rows(part, 0)
        return send(
            tx2.at[here, rows],
            rx2.at[there, rows],
            s2.at[part * SEQ + here],
            r2.at[part * SEQ + there],
            (device, t, r),
        )

    def local_copy(pair, part):
        return local_send(pair, s, part, pair)

    def local_arrival(source, part):
        return local_send(source, source, part, source)

    def prefix_copy(target, part):
        return prefix_send(target, s, part, target)

    def prefix_arrival(pair, part):
        return prefix_send(pair, pair, part, pair)

    length = len_ref[0]
    live = s * ROWS + iota((ROWS, LANES), 0) < length
    low = iota((ROWS, LANES), 1) < 64

    steps = jnp.concatenate(
        [st_ref[0].astype(F32), jnp.zeros((LANES - 32, ROWS), F32)], axis=0
    ).T
    rates = jnp.concatenate([rate_ref[...], jnp.zeros((1, LANES - 32), F32)], axis=1)
    steps = jnp.where(live, steps, 0.0)
    causal = iota((ROWS, ROWS), 0) >= iota((ROWS, ROWS), 1)
    logs = jnp.dot(
        causal.astype(F32),
        steps * rates * -LOG2E,
        precision=lax.Precision.HIGHEST,
        preferred_element_type=F32,
    )
    used = steps > 0.0
    less = jnp.where(used, logs - jnp.log(jnp.where(used, steps, 1.0)) * LOG2E, 1e9)
    log_ref[...] = logs
    weights = jnp.exp2(logs[ROWS - 1 :, :] - less)
    decays = jnp.exp2(logs[ROWS - 8 :, :])
    mt_ref[...] = less.T

    for copy in fetched[:2]:
        copy.wait()
    keys = jnp.where(live, k_ref[...].astype(F32), 0.0)
    values = jnp.where(live, v_ref[...].astype(F32), 0.0)
    flipped = values.T.astype(BF16)
    hkt[0, 0] = keys.astype(BF16)
    hkt[0, 1] = values.astype(BF16)
    kvo[z, 0] = keys.astype(BF16)
    kvo[z, 1, :LANES] = flipped[:, :LANES]
    kvo[z, 1, LANES:] = flipped[:, LANES:]
    pl.semaphore_wait(barrier, SEQ - 1 + 4)
    up_copy(z).start()
    down_copy(z).start()

    @pl.when(row == 0)
    def _():
        cross_copy(z).start()

    kv_hop(0).start()

    for copy in fetched[2:4]:
        copy.wait()
    bt_ref[...] = b_ref[...].astype(F32).T.astype(BF16)
    which = iota((16, LANES), 0)
    for pair in range(SEQ):
        cols = slice(pair * LANES, (pair + 1) * LANES)
        one, two = 2 * pair, 2 * pair + 1
        weight = jnp.where(low, weights[:, one : one + 1], weights[:, two : two + 1])
        xw_ref[:, cols] = (x_ref[:, cols].astype(F32) * weight).astype(BF16)
        decay = jnp.where(low[:1], decays[7:8, one : one + 1], decays[7:8, two : two + 1])
        high = decay.astype(BF16).astype(F32)
        middle = (decay - high).astype(BF16).astype(F32)
        rest = decay - high - middle
        tx1[pair, :HEAD, :] = jnp.where(
            which == 0, high, jnp.where(which == 1, middle, jnp.where(which == 2, rest, 0.0))
        ).astype(BF16)
    for twice in range(RING):
        fresh = jnp.dot(
            bt_ref[...],
            xw_ref[:, twice * 2 * LANES : (twice + 1) * 2 * LANES],
            preferred_element_type=F32,
        ).astype(BF16)
        tx1[2 * twice, HEAD:, :] = fresh[:, :LANES]
        tx1[2 * twice + 1, HEAD:, :] = fresh[:, LANES:]
    groups = [(0, 1, 9), (0, 9, SEQ), (1, 1, 9), (1, 9, SEQ)]

    def send_group(index):
        part, first, end = groups[index]
        for k in range(first, end):
            local_copy(lax.rem(s + k, SEQ), part).start()

    send_group(0)
    rx1[s] = tx1[s]

    fetched[4].wait()
    gm_ref[...] = jnp.where(
        causal,
        lax.dot_general(
            c_ref[...], b_ref[...], (((1,), (1,)), ((), ())), preferred_element_type=F32
        ),
        0.0,
    )
    for copy in fetched[5:]:
        copy.wait()
    key_xor = own_ref[0]
    skips = jnp.broadcast_to(
        jnp.concatenate([skip_ref[...], jnp.zeros((1, LANES - 32), F32)], axis=1), (8, LANES)
    )

    def within(four):
        shift = lax.rem(LANES - 8 * four, LANES)
        turned = pltpu.roll(log_ref[...], shift, axis=1)
        gains = pltpu.roll(skips, shift, axis=1)
        table = mt_ref[pl.ds(pl.multiple_of(8 * four, 8), 8), :]
        for j in range(4):
            cols = pl.ds(pl.multiple_of((4 * four + j) * LANES, LANES), LANES)
            heads = [2 * j, 2 * j + 1]
            columns = [jnp.broadcast_to(turned[:, i : i + 1], (ROWS, LANES)) for i in heads]
            lines = [table[i : i + 1, :] for i in heads]
            x = x_ref[:, cols].astype(F32)
            halves = [jnp.where(low, x, 0.0).astype(BF16), jnp.where(low, 0.0, x).astype(BF16)]

            def mix(head, below, right):
                rows, over = slice(below, below + 128), slice(right, right + 128)
                spread = columns[head][rows] - lines[head][:, over]
                return (gm_ref[rows, over] * jnp.exp2(spread)).astype(BF16)

            gain = jnp.where(
                low[:1], gains[:1, heads[0] : heads[0] + 1], gains[:1, heads[1] : heads[1] + 1]
            )
            skipped = gain * x
            upper = jnp.dot(
                jnp.concatenate([mix(0, 0, 0), mix(1, 0, 0)], axis=1),
                jnp.concatenate([halves[0][:128], halves[1][:128]], axis=0),
                preferred_element_type=F32,
            )
            lower = jnp.dot(
                jnp.concatenate(
                    [mix(0, 128, 0), mix(0, 128, 128), mix(1, 128, 0), mix(1, 128, 128)], axis=1
                ),
                jnp.concatenate(halves, axis=0),
                preferred_element_type=F32,
            )
            y_ref[:128, cols] = upper + skipped[:128]
            y_ref[128:, cols] = lower + skipped[128:]
            el_ref[:, cols] = jnp.exp2(jnp.where(low, columns[0], columns[1]))
            gate = g_ref[:, cols].astype(F32)
            sg_ref[:, cols] = gate / (1.0 + jnp.exp(-gate))

    def routed(level, arrived, held):
        bit = lax.rem(key_xor // (1 << (level - 1)), 2)
        take = jnp.broadcast_to(bit, arrived.shape) == 1
        return jnp.where(take, arrived.astype(F32), held.astype(F32)).astype(BF16)

    def kv_step(level):
        kv_hop(level).wait_recv()
        for part in range(2):
            moved = hkr[level, part]
            if level > 0:
                moved = routed(level, moved, hkt[level, part])
            if level < 3:
                hkt[level + 1, part] = moved
            else:
                dk_ref[0, part] = moved
        if level < 3:
            kv_hop(level + 1).start()

    def ring_turn(four, carry):
        within(four)
        for j in range(2):
            h = 2 * four + j
            cols = pl.ds(pl.multiple_of(h * LANES, LANES), LANES)
            qt_ref[h] = q_ref[:, cols].astype(F32).T.astype(BF16)
        before = lax.rem(z - four - 1 + RING, RING)
        after = lax.rem(z + four + 1, RING)
        up_copy(before).wait_recv()

        @pl.when(four < 3)
        def _():
            up_copy(before).start()
            down_copy(after).wait_recv()

        @pl.when(four < 2)
        def _():
            down_copy(after).start()

        for index in range(1, 4):

            @pl.when(four == index - 1)
            def _():
                send_group(index)

        @pl.when(row == 0)
        def _():
            cross_copy(before).start()

            @pl.when(four < 3)
            def _():
                cross_copy(after).start()

        for level in range(4):

            @pl.when(four == level)
            def _():
                kv_step(level)

        return carry

    lax.fori_loop(0, 4, ring_turn, 0)

    state_ref[...] = jnp.zeros((STATE, LANES), F32)

    def scan(part):
        rows = slice(part * HALF, (part + 1) * HALF)
        stored = slice(HEAD + part * HALF, HEAD + (part + 1) * HALF)

        def turn(i, carry):
            now = state_ref[rows]
            tx2[i, rows] = now.astype(BF16)

            @pl.when(i == s)
            def _():
                rx2[s, rows] = now.astype(BF16)

            @pl.when(i != s)
            def _():
                prefix_copy(i, part).start()
                local_arrival(i, part).wait_recv()

            decay = jnp.sum(rx1[i, :HEAD, :].astype(F32), axis=0, keepdims=True)
            state_ref[rows] = now * decay + rx1[i, stored, :].astype(F32)
            return carry

        lax.fori_loop(0, SEQ, turn, 0)

    scan(0)
    scan(1)
    hst[0] = state_ref[...].astype(BF16)
    state_hop(0).start()

    def state_step(level):
        state_hop(level).wait_recv()
        moved = hsr[level]
        if level > 0:
            moved = routed(level, moved, hst[level])
        if level < 3:
            hst[level + 1] = moved
            state_hop(level + 1).start()
        else:
            ds_ref[0] = moved.astype(F32).T.reshape(2, 64, STATE)

    top_ref[...] = jnp.full(top_ref.shape, -1e30, F32)
    den_ref[...] = jnp.zeros(den_ref.shape, F32)
    acc_ref[...] = jnp.zeros(acc_ref.shape, F32)

    def attend(kv, first, ahead):
        def score(h):
            for w in range(4):
                sc_ref[h % 2, w * ROWS : (w + 1) * ROWS] = jnp.dot(
                    kv[first + w, 0], qt_ref[h], preferred_element_type=F32
                )

        def soften(h):
            scores = sc_ref[h % 2]
            if ahead is not None:
                apart = iota((4 * ROWS, ROWS), 0) - iota((4 * ROWS, ROWS), 1)
                scores = jnp.where(apart <= ahead, scores, -jnp.inf)
            old = top_ref[h]
            new = jnp.maximum(old, jnp.max(scores, axis=0, keepdims=True) * SCORE)
            weight = jnp.exp2(scores * SCORE - new)
            scale = jnp.exp2(old - new)
            wt_ref[h % 2] = weight.astype(BF16)
            den_ref[h] = den_ref[h] * scale + jnp.sum(weight, axis=0, keepdims=True)
            top_ref[h] = new
            return scale

        def mix(h, scale):
            part = 0.0
            for w in range(4):
                flat = kv[first + w, 1]
                part = part + jnp.dot(
                    jnp.concatenate([flat[:LANES], flat[LANES:]], axis=1),
                    wt_ref[h % 2, w * ROWS : (w + 1) * ROWS],
                    preferred_element_type=F32,
                )
            acc_ref[h] = acc_ref[h] * scale + part

        score(0)
        for h in range(HEADS):
            if h + 1 < HEADS:
                score(h + 1)
            mix(h, soften(h))

    def own_row(part, carry):
        @pl.when(z >= 4 * part)
        def _():
            attend(kvo, 4 * part, z * ROWS - part * 4 * ROWS)

        @pl.when(part == 1)
        def _():
            state_step(0)

        return carry

    lax.fori_loop(0, 2, own_row, 0)

    def other_row(part, carry):
        @pl.when(row == 1)
        def _():
            for w in range(4):
                cross_copy(4 * part + w).wait_recv()
            attend(kvx, 4 * part, None)

        @pl.when(part == 1)
        def _():
            state_step(1)

        return carry

    lax.fori_loop(0, 2, other_row, 0)

    for h in range(HEADS):
        attended = (acc_ref[h] / den_ref[h]).T
        ao_ref[0, :, h * LANES : (h + 1) * LANES] = jnp.where(live, attended, 0.0).astype(BF16)

    sq_ref[...] = jnp.zeros((ROWS, LANES), F32)

    def outputs(part):
        rows = slice(part * HALF, (part + 1) * HALF)

        def turn(twice, carry):
            pairs = [lax.rem(s + 2 * twice + j, SEQ) for j in range(2)]

            @pl.when(twice > 0)
            def _():
                prefix_arrival(pairs[0], part).wait_recv()

            prefix_arrival(pairs[1], part).wait_recv()
            carried = jnp.dot(
                c_ref[:, rows],
                jnp.concatenate([rx2[pair, rows] for pair in pairs], axis=1),
                preferred_element_type=F32,
            )
            for j, pair in enumerate(pairs):
                cols = pl.ds(pl.multiple_of(pair * LANES, LANES), LANES)
                mine = carried[:, j * LANES : (j + 1) * LANES]
                total = y_ref[:, cols] + el_ref[:, cols] * mine
                if part == 0:
                    y_ref[:, cols] = total
                else:
                    gated = total.astype(BF16).astype(F32) * sg_ref[:, cols]
                    y_ref[:, cols] = gated
                    sq_ref[...] += gated * gated
            return carry

        lax.fori_loop(0, RING, turn, 0)

    outputs(0)
    state_step(2)
    outputs(1)
    state_step(3)
    mean = jnp.sum(sq_ref[...], axis=1, keepdims=True) * (1.0 / 2048.0)
    sq_ref[...] = jnp.where(live, lax.rsqrt(mean + 1e-05), 0.0)

    for k in range(1, SEQ):
        for part in range(2):
            local_copy(lax.rem(s + k, SEQ), part).wait_send()
            prefix_copy(lax.rem(s + k, SEQ), part).wait_send()
    for k in range(4):
        up_copy(lax.rem(z - k + RING, RING)).wait_send()
    for k in range(3):
        down_copy(lax.rem(z + k, RING)).wait_send()

    @pl.when(row == 0)
    def _():
        for slot in range(RING):
            cross_copy(slot).wait_send()

    for level in range(4):
        kv_hop(level).wait_send()
        state_hop(level).wait_send()


def finish(y_ref, factor_ref, gain_ref, ao_in, ds_in, dk_in, mo_ref, ao_ref, ds_ref, dk_ref):
    for i in range(y_ref.shape[1] // LANES):
        cols = slice(i * LANES, (i + 1) * LANES)
        mo_ref[0, :, cols] = (y_ref[:, cols] * factor_ref[...] * gain_ref[:, cols]).astype(BF16)
    ao_ref[...] = ao_in[...]
    ds_ref[...] = ds_in[...]
    dk_ref[...] = dk_in[...]


def on_device(
    prompt_length,
    owner_map,
    queries,
    key_rows,
    value_matrix,
    ssm_input,
    gate_input,
    step_sizes,
    decay_rate,
    skip_gain,
    write_proj,
    read_proj,
    norm_gain,
):
    smem = pl.BlockSpec(memory_space=pltpu.SMEM)
    vmem = pl.BlockSpec(memory_space=pltpu.VMEM)
    hbm = pl.BlockSpec(memory_space=pltpu.HBM)
    dma = pltpu.SemaphoreType.DMA
    wide = pltpu.VMEM((ROWS, SEQ * LANES), F32)
    tokens = pltpu.VMEM((ROWS, SEQ * LANES), BF16)
    square = pltpu.VMEM((ROWS, LANES), F32)
    narrow = pltpu.VMEM((ROWS, LANES), BF16)
    group = pltpu.VMEM((ROWS, STATE), BF16)
    block = pltpu.VMEM((RING, 2, ROWS, LANES), BF16)
    gated, factor, attn, state, kv = pl.pallas_call(
        kernel,
        name="prefill",
        out_shape=(
            jax.ShapeDtypeStruct((ROWS, 2048), F32),
            jax.ShapeDtypeStruct((ROWS, LANES), F32),
            jax.ShapeDtypeStruct((1, ROWS, 1024), BF16),
            jax.ShapeDtypeStruct((1, 2, 64, STATE), F32),
            jax.ShapeDtypeStruct((1, 2, ROWS, LANES), BF16),
        ),
        in_specs=[smem, smem, hbm, hbm, hbm, hbm, hbm, vmem, vmem, vmem, hbm, hbm],
        out_specs=(vmem,) * 5,
        scratch_shapes=[
            pltpu.VMEM((ROWS, 1024), BF16),
            narrow,
            narrow,
            tokens,
            tokens,
            group,
            group,
            block,
            block,
            pltpu.VMEM((SEQ, HEAD + STATE, LANES), BF16),
            pltpu.VMEM((SEQ, HEAD + STATE, LANES), BF16),
            pltpu.VMEM((SEQ, STATE, LANES), BF16),
            pltpu.VMEM((SEQ, STATE, LANES), BF16),
            pltpu.VMEM((4, 2, ROWS, LANES), BF16),
            pltpu.VMEM((4, 2, ROWS, LANES), BF16),
            pltpu.VMEM((4, STATE, LANES), BF16),
            pltpu.VMEM((4, STATE, LANES), BF16),
            square,
            pltpu.VMEM((LANES, ROWS), F32),
            group,
            tokens,
            pltpu.VMEM((ROWS, ROWS), F32),
            wide,
            wide,
            pltpu.VMEM((HEADS, LANES, ROWS), BF16),
            pltpu.VMEM((2, 4 * ROWS, ROWS), F32),
            pltpu.VMEM((2, 4 * ROWS, ROWS), BF16),
            pltpu.VMEM((HEADS, 1, ROWS), F32),
            pltpu.VMEM((HEADS, 1, ROWS), F32),
            pltpu.VMEM((HEADS, LANES, ROWS), F32),
            pltpu.VMEM((STATE, LANES), F32),
            dma((7,)),
            dma((2 * SEQ,)),
            dma((2 * SEQ,)),
            dma((2 * SEQ,)),
            dma((2 * SEQ,)),
            dma((RING,)),
            dma((RING,)),
            dma((RING,)),
            dma((RING,)),
            dma((RING,)),
            dma((4,)),
            dma((4,)),
            dma((4,)),
            dma((4,)),
        ],
        compiler_params=pltpu.CompilerParams(
            collective_id=0, has_side_effects=True, vmem_limit_bytes=63 * 2**20
        ),
    )(
        prompt_length,
        owner_map,
        queries,
        key_rows,
        value_matrix,
        ssm_input,
        gate_input,
        jnp.swapaxes(step_sizes, 1, 2),
        decay_rate.reshape(1, 32),
        skip_gain.reshape(1, 32),
        write_proj,
        read_proj,
    )
    part = 1024
    passed = [
        pl.BlockSpec((1, ROWS, 512), lambda i: (0, 0, i)),
        pl.BlockSpec((1, 2, 32, STATE), lambda i: (0, 0, i, 0)),
        pl.BlockSpec((1, 2, 128, LANES), lambda i: (0, 0, i, 0)),
    ]
    return pl.pallas_call(
        finish,
        name="finish",
        grid=(2048 // part,),
        out_shape=(
            jax.ShapeDtypeStruct((1, ROWS, 2048), BF16),
            jax.ShapeDtypeStruct(attn.shape, attn.dtype),
            jax.ShapeDtypeStruct(state.shape, state.dtype),
            jax.ShapeDtypeStruct(kv.shape, kv.dtype),
        ),
        in_specs=[
            pl.BlockSpec((ROWS, part), lambda i: (0, i)),
            pl.BlockSpec((ROWS, LANES), lambda i: (0, 0)),
            pl.BlockSpec((1, part), lambda i: (0, i)),
            *passed,
        ],
        out_specs=(pl.BlockSpec((1, ROWS, part), lambda i: (0, 0, i)), *passed),
    )(gated, factor, norm_gain.reshape(1, 2048), attn, state, kv)


def solution(mesh):
    tokens = P("role", "seq", "tp")
    in_specs = (
        P("role"),
        P(),
        tokens,
        tokens,
        tokens,
        tokens,
        tokens,
        tokens,
        P("tp"),
        P("tp"),
        tokens,
        tokens,
        P("tp"),
    )
    out_specs = (
        tokens,
        tokens,
        P("role", ("tp", "seq"), None, None),
        P("role", None, "seq", "tp"),
    )
    return jax.shard_map(
        on_device, mesh=mesh, in_specs=in_specs, out_specs=out_specs, check_vma=False
    )
```

```python
import jax
import jax.numpy as jnp
from jax import lax
from jax.experimental import pallas as pl
from jax.experimental.pallas import tpu as pltpu
from jax.sharding import PartitionSpec as P

MESH = pl.DeviceIdType.MESH
LOG2E = 1.4426950408889634
SCORE = 128**-0.5 * LOG2E
ROWS = 256
LANES = 128
SEQ = 16
RING = 8
HEADS = 8
STATE = 256
HEAD = 16
HALF = STATE // 2
F32 = jnp.float32
BF16 = jnp.bfloat16


def iota(shape, dim):
    return lax.broadcasted_iota(jnp.int32, shape, dim)


def kernel(
    len_ref,
    own_ref,
    q_hbm,
    k_hbm,
    v_hbm,
    x_hbm,
    g_hbm,
    st_ref,
    rate_ref,
    skip_ref,
    b_hbm,
    c_hbm,
    y_ref,
    sq_ref,
    ao_ref,
    ds_ref,
    dk_ref,
    q_ref,
    k_ref,
    v_ref,
    x_ref,
    g_ref,
    b_ref,
    c_ref,
    kvo,
    kvx,
    tx1,
    rx1,
    tx2,
    rx2,
    hkt,
    hkr,
    hst,
    hsr,
    log_ref,
    mt_ref,
    bt_ref,
    xw_ref,
    gm_ref,
    el_ref,
    sg_ref,
    qt_ref,
    sc_ref,
    wt_ref,
    top_ref,
    den_ref,
    acc_ref,
    state_ref,
    loads,
    s1,
    r1,
    s2,
    r2,
    up,
    down,
    ro,
    sx,
    rx,
    sk,
    rk,
    sf,
    rf,
):
    s, t, r = lax.axis_index("seq"), lax.axis_index("tp"), lax.axis_index("role")
    row = s // RING
    z = lax.rem(s, RING)
    across = (lax.rem(s + RING, SEQ), t, r)

    fetched = [
        pltpu.make_async_copy(src.at[0], dst, loads.at[i])
        for i, (src, dst) in enumerate(
            [
                (k_hbm, k_ref),
                (v_hbm, v_ref),
                (b_hbm, b_ref),
                (x_hbm, x_ref),
                (c_hbm, c_ref),
                (g_hbm, g_ref),
                (q_hbm, q_ref),
            ]
        )
    ]
    for copy in fetched[:4]:
        copy.start()

    def on_ring(step):
        return (row * RING + lax.rem(z + step + RING, RING), t, r)

    def owner_hop(level):
        if level == 0:
            return (s, t, 1 - r)
        width = 1 << (level - 1)
        return (s, t + width * (1 - 2 * lax.rem(t // width, 2)), r)

    def send(src, dst, ssem, rsem, device):
        return pltpu.make_async_remote_copy(
            src, dst, ssem, rsem, device_id=device, device_id_type=MESH
        )

    barrier = pltpu.get_barrier_semaphore()
    for k in range(1, SEQ):
        pl.semaphore_signal(
            barrier, inc=1, device_id=(lax.rem(s + k, SEQ), t, r), device_id_type=MESH
        )
    for level in range(4):
        pl.semaphore_signal(barrier, inc=1, device_id=owner_hop(level), device_id_type=MESH)

    def up_copy(slot):
        return send(kvo.at[slot], kvo.at[slot], up.at[slot], ro.at[slot], on_ring(1))

    def down_copy(slot):
        return send(kvo.at[slot], kvo.at[slot], down.at[slot], ro.at[slot], on_ring(-1))

    def cross_copy(slot):
        return send(kvo.at[slot], kvx.at[slot], sx.at[slot], rx.at[slot], across)

    def kv_hop(level):
        return send(
            hkt.at[level], hkr.at[level], sk.at[level], rk.at[level], owner_hop(level)
        )

    def state_hop(level):
        return send(
            hst.at[level], hsr.at[level], sf.at[level], rf.at[level], owner_hop(level)
        )

    def part_rows(part, first):
        return pl.ds(first + part * HALF, HALF) if part else pl.ds(0, first + HALF)

    def local_send(here, there, part, device):
        rows = part_rows(part, HEAD)
        return send(
            tx1.at[here, rows],
            rx1.at[there, rows],
            s1.at[part * SEQ + here],
            r1.at[part * SEQ + there],
            (device, t, r),
        )

    def prefix_send(here, there, part, device):
        rows = part_rows(part, 0)
        return send(
            tx2.at[here, rows],
            rx2.at[there, rows],
            s2.at[part * SEQ + here],
            r2.at[part * SEQ + there],
            (device, t, r),
        )

    def local_copy(pair, part):
        return local_send(pair, s, part, pair)

    def local_arrival(source, part):
        return local_send(source, source, part, source)

    def prefix_copy(target, part):
        return prefix_send(target, s, part, target)

    def prefix_arrival(pair, part):
        return prefix_send(pair, pair, part, pair)

    length = len_ref[0]
    live = s * ROWS + iota((ROWS, LANES), 0) < length
    low = iota((ROWS, LANES), 1) < 64

    steps = jnp.concatenate(
        [st_ref[0].astype(F32), jnp.zeros((LANES - 32, ROWS), F32)], axis=0
    ).T
    rates = jnp.concatenate([rate_ref[...], jnp.zeros((1, LANES - 32), F32)], axis=1)
    steps = jnp.where(live, steps, 0.0)
    causal = iota((ROWS, ROWS), 0) >= iota((ROWS, ROWS), 1)
    logs = jnp.dot(
        causal.astype(F32),
        steps * rates * -LOG2E,
        precision=lax.Precision.HIGHEST,
        preferred_element_type=F32,
    )
    used = steps > 0.0
    less = jnp.where(used, logs - jnp.log(jnp.where(used, steps, 1.0)) * LOG2E, 1e9)
    log_ref[...] = logs
    weights = jnp.exp2(logs[ROWS - 1 :, :] - less)
    decays = jnp.exp2(logs[ROWS - 8 :, :])
    mt_ref[...] = less.T

    for copy in fetched[:2]:
        copy.wait()
    keys = jnp.where(live, k_ref[...].astype(F32), 0.0)
    values = jnp.where(live, v_ref[...].astype(F32), 0.0)
    flipped = values.T.astype(BF16)
    hkt[0, 0] = keys.astype(BF16)
    hkt[0, 1] = values.astype(BF16)
    kvo[z, 0] = keys.astype(BF16)
    kvo[z, 1, :LANES] = flipped[:, :LANES]
    kvo[z, 1, LANES:] = flipped[:, LANES:]
    for copy in fetched[2:4]:
        copy.wait()
    for copy in fetched[4:]:
        copy.start()
    bt_ref[...] = b_ref[...].astype(F32).T.astype(BF16)
    which = iota((16, LANES), 0)
    for pair in range(SEQ):
        cols = slice(pair * LANES, (pair + 1) * LANES)
        one, two = 2 * pair, 2 * pair + 1
        weight = jnp.where(low, weights[:, one : one + 1], weights[:, two : two + 1])
        xw_ref[:, cols] = (x_ref[:, cols].astype(F32) * weight).astype(BF16)
        decay = jnp.where(low[:1], decays[7:8, one : one + 1], decays[7:8, two : two + 1])
        high = decay.astype(BF16).astype(F32)
        middle = (decay - high).astype(BF16).astype(F32)
        rest = decay - high - middle
        tx1[pair, :HEAD, :] = jnp.where(
            which == 0, high, jnp.where(which == 1, middle, jnp.where(which == 2, rest, 0.0))
        ).astype(BF16)
    for twice in range(RING):
        fresh = jnp.dot(
            bt_ref[...],
            xw_ref[:, twice * 2 * LANES : (twice + 1) * 2 * LANES],
            preferred_element_type=F32,
        ).astype(BF16)
        tx1[2 * twice, HEAD:, :] = fresh[:, :LANES]
        tx1[2 * twice + 1, HEAD:, :] = fresh[:, LANES:]
    pl.semaphore_wait(barrier, SEQ - 1 + 4)
    up_copy(z).start()
    down_copy(z).start()

    @pl.when(row == 0)
    def _():
        cross_copy(z).start()

    kv_hop(0).start()

    groups = [(0, 1, 9), (0, 9, SEQ), (1, 1, 9), (1, 9, SEQ)]

    def send_group(index):
        part, first, end = groups[index]
        for k in range(first, end):
            local_copy(lax.rem(s + k, SEQ), part).start()

    send_group(0)
    rx1[s] = tx1[s]

    fetched[4].wait()
    gm_ref[...] = jnp.where(
        causal,
        lax.dot_general(
            c_ref[...], b_ref[...], (((1,), (1,)), ((), ())), preferred_element_type=F32
        ),
        0.0,
    )
    for copy in fetched[5:]:
        copy.wait()
    key_xor = own_ref[0]
    skips = jnp.broadcast_to(
        jnp.concatenate([skip_ref[...], jnp.zeros((1, LANES - 32), F32)], axis=1), (8, LANES)
    )

    def within(four):
        shift = lax.rem(LANES - 8 * four, LANES)
        turned = pltpu.roll(log_ref[...], shift, axis=1)
        gains = pltpu.roll(skips, shift, axis=1)
        table = mt_ref[pl.ds(pl.multiple_of(8 * four, 8), 8), :]
        for j in range(4):
            cols = pl.ds(pl.multiple_of((4 * four + j) * LANES, LANES), LANES)
            heads = [2 * j, 2 * j + 1]
            columns = [jnp.broadcast_to(turned[:, i : i + 1], (ROWS, LANES)) for i in heads]
            lines = [table[i : i + 1, :] for i in heads]
            x = x_ref[:, cols].astype(F32)
            halves = [jnp.where(low, x, 0.0).astype(BF16), jnp.where(low, 0.0, x).astype(BF16)]

            def mix(head, below, right):
                rows, over = slice(below, below + 128), slice(right, right + 128)
                spread = columns[head][rows] - lines[head][:, over]
                return (gm_ref[rows, over] * jnp.exp2(spread)).astype(BF16)

            gain = jnp.where(
                low[:1], gains[:1, heads[0] : heads[0] + 1], gains[:1, heads[1] : heads[1] + 1]
            )
            skipped = gain * x
            upper = jnp.dot(
                jnp.concatenate([mix(0, 0, 0), mix(1, 0, 0)], axis=1),
                jnp.concatenate([halves[0][:128], halves[1][:128]], axis=0),
                preferred_element_type=F32,
            )
            lower = jnp.dot(
                jnp.concatenate(
                    [mix(0, 128, 0), mix(0, 128, 128), mix(1, 128, 0), mix(1, 128, 128)], axis=1
                ),
                jnp.concatenate(halves, axis=0),
                preferred_element_type=F32,
            )
            y_ref[:128, cols] = upper + skipped[:128]
            y_ref[128:, cols] = lower + skipped[128:]
            el_ref[:, cols] = jnp.exp2(jnp.where(low, columns[0], columns[1]))
            gate = g_ref[:, cols].astype(F32)
            sg_ref[:, cols] = gate / (1.0 + jnp.exp(-gate))

    def routed(level, arrived, held):
        bit = lax.rem(key_xor // (1 << (level - 1)), 2)
        take = jnp.broadcast_to(bit, arrived.shape) == 1
        return jnp.where(take, arrived.astype(F32), held.astype(F32)).astype(BF16)

    def kv_step(level):
        kv_hop(level).wait_recv()
        for part in range(2):
            moved = hkr[level, part]
            if level > 0:
                moved = routed(level, moved, hkt[level, part])
            if level < 3:
                hkt[level + 1, part] = moved
            else:
                dk_ref[0, part] = moved
        if level < 3:
            kv_hop(level + 1).start()

    state_ref[...] = jnp.zeros((STATE, LANES), F32)

    def scan(part):
        rows = slice(part * HALF, (part + 1) * HALF)
        stored = slice(HEAD + part * HALF, HEAD + (part + 1) * HALF)

        def turn(i, carry):
            now = state_ref[rows]
            tx2[i, rows] = now.astype(BF16)

            @pl.when(i == s)
            def _():
                rx2[s, rows] = now.astype(BF16)

            @pl.when(i != s)
            def _():
                prefix_copy(i, part).start()
                local_arrival(i, part).wait_recv()

            decay = jnp.sum(rx1[i, :HEAD, :].astype(F32), axis=0, keepdims=True)
            state_ref[rows] = now * decay + rx1[i, stored, :].astype(F32)
            return carry

        lax.fori_loop(0, SEQ, turn, 0)

    def ring_turn(four, carry):
        within(four)
        for j in range(2):
            h = 2 * four + j
            cols = pl.ds(pl.multiple_of(h * LANES, LANES), LANES)
            qt_ref[h] = q_ref[:, cols].astype(F32).T.astype(BF16)
        @pl.when(four == 3)
        def _():
            scan(0)

        before = lax.rem(z - four - 1 + RING, RING)
        after = lax.rem(z + four + 1, RING)
        up_copy(before).wait_recv()

        @pl.when(four < 3)
        def _():
            up_copy(before).start()
            down_copy(after).wait_recv()

        @pl.when(four < 2)
        def _():
            down_copy(after).start()

        for index in range(1, 4):

            @pl.when(four == index - 1)
            def _():
                send_group(index)

        @pl.when(row == 0)
        def _():
            cross_copy(before).start()

            @pl.when(four < 3)
            def _():
                cross_copy(after).start()

        for level in range(4):

            @pl.when(four == level)
            def _():
                kv_step(level)

        return carry

    lax.fori_loop(0, 4, ring_turn, 0)

    scan(1)
    hst[0] = state_ref[...].astype(BF16)
    state_hop(0).start()

    def state_step(level):
        state_hop(level).wait_recv()
        moved = hsr[level]
        if level > 0:
            moved = routed(level, moved, hst[level])
        if level < 3:
            hst[level + 1] = moved
            state_hop(level + 1).start()
        else:
            ds_ref[0] = moved.astype(F32).T.reshape(2, 64, STATE)

    top_ref[...] = jnp.full(top_ref.shape, -1e30, F32)
    den_ref[...] = jnp.zeros(den_ref.shape, F32)
    acc_ref[...] = jnp.zeros(acc_ref.shape, F32)

    def attend(kv, first, ahead):
        def score(h):
            for w in range(4):
                sc_ref[h % 2, w * ROWS : (w + 1) * ROWS] = jnp.dot(
                    kv[first + w, 0], qt_ref[h], preferred_element_type=F32
                )

        def soften(h):
            scores = sc_ref[h % 2]
            if ahead is not None:
                apart = iota((4 * ROWS, ROWS), 0) - iota((4 * ROWS, ROWS), 1)
                scores = jnp.where(apart <= ahead, scores, -jnp.inf)
            old = top_ref[h]
            new = jnp.maximum(old, jnp.max(scores, axis=0, keepdims=True) * SCORE)
            weight = jnp.exp2(scores * SCORE - new)
            scale = jnp.exp2(old - new)
            wt_ref[h % 2] = weight.astype(BF16)
            den_ref[h] = den_ref[h] * scale + jnp.sum(weight, axis=0, keepdims=True)
            top_ref[h] = new
            return scale

        def mix(h, scale):
            part = 0.0
            for w in range(4):
                flat = kv[first + w, 1]
                part = part + jnp.dot(
                    jnp.concatenate([flat[:LANES], flat[LANES:]], axis=1),
                    wt_ref[h % 2, w * ROWS : (w + 1) * ROWS],
                    preferred_element_type=F32,
                )
            acc_ref[h] = acc_ref[h] * scale + part

        score(0)
        for h in range(HEADS):
            if h + 1 < HEADS:
                score(h + 1)
            mix(h, soften(h))

    def own_row(part, carry):
        @pl.when(z >= 4 * part)
        def _():
            attend(kvo, 4 * part, z * ROWS - part * 4 * ROWS)

        @pl.when(part == 1)
        def _():
            state_step(0)

        return carry

    lax.fori_loop(0, 2, own_row, 0)

    def other_row(part, carry):
        @pl.when(row == 1)
        def _():
            for w in range(4):
                cross_copy(4 * part + w).wait_recv()
            attend(kvx, 4 * part, None)

        @pl.when(part == 1)
        def _():
            state_step(1)

        return carry

    lax.fori_loop(0, 2, other_row, 0)

    for h in range(HEADS):
        attended = (acc_ref[h] / den_ref[h]).T
        ao_ref[0, :, h * LANES : (h + 1) * LANES] = jnp.where(live, attended, 0.0).astype(BF16)

    sq_ref[...] = jnp.zeros((ROWS, LANES), F32)

    def outputs(part):
        rows = slice(part * HALF, (part + 1) * HALF)

        def turn(twice, carry):
            pairs = [lax.rem(s + 2 * twice + j, SEQ) for j in range(2)]

            @pl.when(twice > 0)
            def _():
                prefix_arrival(pairs[0], part).wait_recv()

            prefix_arrival(pairs[1], part).wait_recv()
            carried = jnp.dot(
                c_ref[:, rows],
                jnp.concatenate([rx2[pair, rows] for pair in pairs], axis=1),
                preferred_element_type=F32,
            )
            for j, pair in enumerate(pairs):
                cols = pl.ds(pl.multiple_of(pair * LANES, LANES), LANES)
                mine = carried[:, j * LANES : (j + 1) * LANES]
                total = y_ref[:, cols] + el_ref[:, cols] * mine
                if part == 0:
                    y_ref[:, cols] = total
                else:
                    gated = total.astype(BF16).astype(F32) * sg_ref[:, cols]
                    y_ref[:, cols] = gated
                    sq_ref[...] += gated * gated
            return carry

        lax.fori_loop(0, RING, turn, 0)

    outputs(0)
    state_step(2)
    outputs(1)
    state_step(3)
    mean = jnp.sum(sq_ref[...], axis=1, keepdims=True) * (1.0 / 2048.0)
    sq_ref[...] = jnp.where(live, lax.rsqrt(mean + 1e-05), 0.0)

    for k in range(1, SEQ):
        for part in range(2):
            local_copy(lax.rem(s + k, SEQ), part).wait_send()
            prefix_copy(lax.rem(s + k, SEQ), part).wait_send()
    for k in range(4):
        up_copy(lax.rem(z - k + RING, RING)).wait_send()
    for k in range(3):
        down_copy(lax.rem(z + k, RING)).wait_send()

    @pl.when(row == 0)
    def _():
        for slot in range(RING):
            cross_copy(slot).wait_send()

    for level in range(4):
        kv_hop(level).wait_send()
        state_hop(level).wait_send()


def finish(y_ref, factor_ref, gain_ref, ao_in, ds_in, dk_in, mo_ref, ao_ref, ds_ref, dk_ref):
    for i in range(y_ref.shape[1] // LANES):
        cols = slice(i * LANES, (i + 1) * LANES)
        mo_ref[0, :, cols] = (y_ref[:, cols] * factor_ref[...] * gain_ref[:, cols]).astype(BF16)
    ao_ref[...] = ao_in[...]
    ds_ref[...] = ds_in[...]
    dk_ref[...] = dk_in[...]


def on_device(
    prompt_length,
    owner_map,
    queries,
    key_rows,
    value_matrix,
    ssm_input,
    gate_input,
    step_sizes,
    decay_rate,
    skip_gain,
    write_proj,
    read_proj,
    norm_gain,
):
    smem = pl.BlockSpec(memory_space=pltpu.SMEM)
    vmem = pl.BlockSpec(memory_space=pltpu.VMEM)
    hbm = pl.BlockSpec(memory_space=pltpu.HBM)
    dma = pltpu.SemaphoreType.DMA
    wide = pltpu.VMEM((ROWS, SEQ * LANES), F32)
    tokens = pltpu.VMEM((ROWS, SEQ * LANES), BF16)
    square = pltpu.VMEM((ROWS, LANES), F32)
    narrow = pltpu.VMEM((ROWS, LANES), BF16)
    group = pltpu.VMEM((ROWS, STATE), BF16)
    block = pltpu.VMEM((RING, 2, ROWS, LANES), BF16)
    gated, factor, attn, state, kv = pl.pallas_call(
        kernel,
        name="prefill",
        out_shape=(
            jax.ShapeDtypeStruct((ROWS, 2048), F32),
            jax.ShapeDtypeStruct((ROWS, LANES), F32),
            jax.ShapeDtypeStruct((1, ROWS, 1024), BF16),
            jax.ShapeDtypeStruct((1, 2, 64, STATE), F32),
            jax.ShapeDtypeStruct((1, 2, ROWS, LANES), BF16),
        ),
        in_specs=[smem, smem, hbm, hbm, hbm, hbm, hbm, vmem, vmem, vmem, hbm, hbm],
        out_specs=(vmem,) * 5,
        scratch_shapes=[
            pltpu.VMEM((ROWS, 1024), BF16),
            narrow,
            narrow,
            tokens,
            tokens,
            group,
            group,
            block,
            block,
            pltpu.VMEM((SEQ, HEAD + STATE, LANES), BF16),
            pltpu.VMEM((SEQ, HEAD + STATE, LANES), BF16),
            pltpu.VMEM((SEQ, STATE, LANES), BF16),
            pltpu.VMEM((SEQ, STATE, LANES), BF16),
            pltpu.VMEM((4, 2, ROWS, LANES), BF16),
            pltpu.VMEM((4, 2, ROWS, LANES), BF16),
            pltpu.VMEM((4, STATE, LANES), BF16),
            pltpu.VMEM((4, STATE, LANES), BF16),
            square,
            pltpu.VMEM((LANES, ROWS), F32),
            group,
            tokens,
            pltpu.VMEM((ROWS, ROWS), F32),
            wide,
            wide,
            pltpu.VMEM((HEADS, LANES, ROWS), BF16),
            pltpu.VMEM((2, 4 * ROWS, ROWS), F32),
            pltpu.VMEM((2, 4 * ROWS, ROWS), BF16),
            pltpu.VMEM((HEADS, 1, ROWS), F32),
            pltpu.VMEM((HEADS, 1, ROWS), F32),
            pltpu.VMEM((HEADS, LANES, ROWS), F32),
            pltpu.VMEM((STATE, LANES), F32),
            dma((7,)),
            dma((2 * SEQ,)),
            dma((2 * SEQ,)),
            dma((2 * SEQ,)),
            dma((2 * SEQ,)),
            dma((RING,)),
            dma((RING,)),
            dma((RING,)),
            dma((RING,)),
            dma((RING,)),
            dma((4,)),
            dma((4,)),
            dma((4,)),
            dma((4,)),
        ],
        compiler_params=pltpu.CompilerParams(
            collective_id=0, has_side_effects=True, vmem_limit_bytes=63 * 2**20
        ),
    )(
        prompt_length,
        owner_map,
        queries,
        key_rows,
        value_matrix,
        ssm_input,
        gate_input,
        jnp.swapaxes(step_sizes, 1, 2),
        decay_rate.reshape(1, 32),
        skip_gain.reshape(1, 32),
        write_proj,
        read_proj,
    )
    part = 1024
    passed = [
        pl.BlockSpec((1, ROWS, 512), lambda i: (0, 0, i)),
        pl.BlockSpec((1, 2, 32, STATE), lambda i: (0, 0, i, 0)),
        pl.BlockSpec((1, 2, 128, LANES), lambda i: (0, 0, i, 0)),
    ]
    return pl.pallas_call(
        finish,
        name="finish",
        grid=(2048 // part,),
        out_shape=(
            jax.ShapeDtypeStruct((1, ROWS, 2048), BF16),
            jax.ShapeDtypeStruct(attn.shape, attn.dtype),
            jax.ShapeDtypeStruct(state.shape, state.dtype),
            jax.ShapeDtypeStruct(kv.shape, kv.dtype),
        ),
        in_specs=[
            pl.BlockSpec((ROWS, part), lambda i: (0, i)),
            pl.BlockSpec((ROWS, LANES), lambda i: (0, 0)),
            pl.BlockSpec((1, part), lambda i: (0, i)),
            *passed,
        ],
        out_specs=(pl.BlockSpec((1, ROWS, part), lambda i: (0, 0, i)), *passed),
    )(gated, factor, norm_gain.reshape(1, 2048), attn, state, kv)


def solution(mesh):
    tokens = P("role", "seq", "tp")
    in_specs = (
        P("role"),
        P(),
        tokens,
        tokens,
        tokens,
        tokens,
        tokens,
        tokens,
        P("tp"),
        P("tp"),
        tokens,
        tokens,
        P("tp"),
    )
    out_specs = (
        tokens,
        tokens,
        P("role", ("tp", "seq"), None, None),
        P("role", None, "seq", "tp"),
    )
    return jax.shard_map(
        on_device, mesh=mesh, in_specs=in_specs, out_specs=out_specs, check_vma=False
    )
```
